256 devices in a mesh: gx: 128 (over x_lo, z, y, core), gz: 2 (over x_hi).
Axes of the slice: x: 4 (x_hi: 2, x_lo: 2; x = x_hi * 2 + x_lo), y: 4, z: 8, core: 2. Of those that a mesh axis runs over, the one named last changes fastest.
Arguments:
- cotangent: float32 [2, 4, 2048, 2048], P(None, 'gz', 'gx'), may hold values from -6 to 6
- damping: float32 [4], P('gz'), may hold values from 0.02 to 0.3
- blending: float32 [4], P('gz'), may hold values from 0.25 to 0.75
Outputs:
- grad_velocity: float32 [2, 4, 2048, 2048], P(None, 'gz', 'gx')
The draws below stay inside these ranges and needn't reach their ends.
All inputs are finite; a program needn't handle non-finite values.
Results may differ from the reference program's by a relative error of at most 0.000096.
Values sent between devices are 32-bit elements; how exact they have to be, the bound alone decides.
A program may use at most 64 MiB of HBM per device.

```python
import math
import jax
import jax.numpy as jnp
from jax import lax

NX = 2048
NY = 2048
NZ = 4


def steps_of(stream_key, shape, split, smallest, largest):
    def one(dim, blocks):
        draws = jax.random.uniform(jax.random.fold_in(jax.random.fold_in(stream_key, 6), dim), (blocks,), jnp.float32, smallest / len(split), largest / len(split))
        return jnp.repeat(jnp.exp(draws), shape[dim] // blocks).reshape((-1,) + (1,) * (len(shape) - dim - 1))

    level = one(*split[0])
    for cut in split[1:]:
        level = level * one(*cut)
    return level


def noise(rng, extent, scale, bound, pieces=(), kind=jnp.bfloat16):
    values = scale * jax.random.normal(rng, extent, jnp.float32)
    if pieces:
        values = values * steps_of(rng, extent, pieces, -0.22, 0.18)
    return jnp.clip(values, -bound, bound).astype(kind)


def setup_inputs(seed: int = 0) -> dict:
    key_of = jax.random.split(jax.random.key(seed), 4)
    return {
        "cotangent": noise(key_of[0], (2, NZ, NX, NY), 1.0, 6.0, ((1, 2), (2, 128)), jnp.float32),
        "damping": jnp.clip(jnp.exp(math.log(0.3) - 2.7080503 * jax.random.uniform(key_of[1], (NZ,), jnp.float32) ** steps_of(key_of[1], (NZ,), ((0, 2),), -0.2, 0.2)), 0.02, 0.3),
        "blending": jnp.clip(0.25 + 0.5 * jax.random.uniform(key_of[2], (NZ,), jnp.float32) ** steps_of(key_of[2], (NZ,), ((0, 2),), -0.2, 0.2), 0.25, 0.75),
    }


def signed_index(count):
    index = jnp.arange(count)
    signed = jnp.where(index < count // 2, index, index - count)
    return jnp.where(index == count // 2, 0, signed)


def reference(cotangent, damping, blending):
    wave_x = signed_index(NX)
    wave_y = signed_index(NY)
    along_x = (2.0 * math.pi / NX) * wave_x.astype(jnp.float32)
    along_y = (2.0 * math.pi / NY) * wave_y.astype(jnp.float32)
    squared = along_x[:, None] ** 2 + along_y[None, :] ** 2
    anchor = (wave_x[:, None] == 0) & (wave_y[None, :] == 0)
    inverse = jnp.where(anchor, 0.0, 1.0 / jnp.where(anchor, 1.0, squared))

    def one_level(pair):
        level_field, rate = pair
        spectra = jnp.fft.fft2(level_field, axes=(-2, -1))
        damper = jnp.exp(-rate * squared)
        inner = along_x[:, None] * spectra[0] + along_y[None, :] * spectra[1]
        first = damper * (spectra[0] - along_x[:, None] * inner * inverse)
        second = damper * (spectra[1] - along_y[None, :] * inner * inverse)
        back = jnp.fft.ifft2(jnp.stack([first, second]), axes=(-2, -1))
        return jnp.real(back).astype(cotangent.dtype)

    levels = lax.map(one_level, (jnp.moveaxis(cotangent, 1, 0), damping))
    projected = jnp.moveaxis(levels, 0, 1)
    carried = (1.0 - blending)[None, :, None, None] * projected
    below = jnp.concatenate([jnp.zeros_like(carried[:, :1]), carried[:, :-1]], axis=1)
    return blending[None, :, None, None] * projected + below
```

```python
import functools
import math

import jax
import jax.numpy as jnp
import numpy as np
from jax import lax
from jax.experimental import pallas as pl
from jax.experimental.pallas import tpu as pltpu
from jax.sharding import PartitionSpec as P

NX = 2048
NY = 2048
CHIPS = 128
LANES = 128
GROUPS = 8
CHUNKS = 2
KEYS = 4 // CHUNKS
ROWS = 2 * KEYS
MESH = pl.DeviceIdType.MESH
F32 = jnp.float32
BF16 = jnp.bfloat16


def split_const(table):
    table = np.asarray(table, np.float32)
    high = table.astype(BF16)
    low = (table - high.astype(np.float32)).astype(BF16)
    return np.stack([high, low])


def wave(numerator, period):
    angle = 2.0 * np.pi * (np.asarray(numerator, np.int64) % period) / period
    return np.cos(angle), np.sin(angle)


@functools.cache
def tables():
    d = np.arange(128)[:, None]
    b = np.arange(128)[None, :]
    groups = []
    for c in range(1, 8):
        cos, sin = wave(b * (c + 16 * d), NY)
        groups.append(np.concatenate([cos, -sin], axis=1))
    main = split_const(np.stack(groups))
    half = np.arange(64)[:, None]
    cos0, sin0 = wave(b * (16 * half), NY)
    cos8, sin8 = wave(b * (8 + 16 * half), NY)
    im0 = -sin0
    im0[0] = 1.0 - 2.0 * (np.arange(128) % 2)
    zero = np.zeros((64, 128))
    packed = np.block([[cos0, zero, im0, zero], [zero, cos8, zero, -sin8]])
    packed = split_const(packed)
    core, x_lo, y, z = np.meshgrid(range(2), range(2), range(4), range(8), indexing="ij")
    slab = (x_lo * 64 + z * 8 + y * 2 + core).reshape(-1)
    k1 = np.arange(128)
    cos, sin = wave(k1[:, None] * slab[None, :], 128)
    slab_fwd = split_const(np.concatenate([cos, sin], axis=1))
    slab_inv = split_const(np.concatenate([cos.T, -sin.T], axis=1))
    lane = np.arange(128)
    cos, sin = wave(k1[:, None] * (lane % 16)[None, :], NX)
    sign = np.where(lane < 64, 1.0, -1.0)[None, :]
    twiddle = np.stack([cos, sin * sign]).astype(np.float32)
    src, dst = lane[:, None], lane[None, :]
    same = (src // 16) % 4 == (dst // 16) % 4
    cos, sin = wave((src % 16) * (dst % 16), 16)
    src_im, dst_im = src // 64, dst // 64
    fwd = np.where(src_im == dst_im, cos, np.where(dst_im == 0, sin, -sin)) * same
    inv = np.where(src_im == dst_im, cos, np.where(dst_im == 0, -sin, sin))
    mix = split_const(np.concatenate([fwd, fwd[:, lane ^ 32]], axis=1))
    row = np.arange(256)[:, None]
    col = np.arange(256)[None, :]
    level_row = (row // 128) * 2 + (row // 16) % 2
    level_col = (col // 128) * 2 + (col // 16) % 2
    same_c = (row // 32) % 2 == (col // 32) % 2
    inv = np.tile(inv, (2, 2)) * same_c
    keep = inv * (level_row == level_col)
    carry = inv * (level_row + 1 == level_col)
    vertical = np.stack([keep, carry]).astype(np.float32)
    return main, packed, slab_fwd, slab_inv, twiddle, mix, vertical


def split(value):
    high = value.astype(BF16)
    low = (value - high.astype(F32)).astype(BF16)
    return high, low


def dot(a, b, dims):
    return lax.dot_general(a, b, (dims, ((), ())), preferred_element_type=F32)


def dot_const_left(table, high, low, dims=((1,), (0,))):
    c_high, c_low = table
    return dot(c_high, high, dims) + (dot(c_low, high, dims) + dot(c_high, low, dims))


def dot_const_right(high, low, table, dims=((1,), (0,))):
    c_high, c_low = table
    return dot(high, c_high, dims) + (dot(low, c_high, dims) + dot(high, c_low, dims))


def kernel(
    x_ref, damp_ref, blend_ref, main_ref, packed_ref, slabf_ref, slabi_ref, twid_ref, mix_ref, vert_ref,
    out_ref,
    fold, yf, sib_f, w1, r1, coef, vmat, w2, r2, own_b, yb, acc_e, acc_o, par,
    core_f_s, core_f_r, chip_f_s, chip_f_r, chip_b_s, chip_b_r, core_b_s, core_b_r, par_s, par_r, self_sem,
):
    gx = lax.axis_index("gx")
    gz = lax.axis_index("gz")
    x_lo, z, y, core = gx // 64, (gx // 8) % 8, (gx // 2) % 4, gx % 2
    x = gz * 2 + x_lo
    me = x * 32 + y * 8 + z
    other = 1 - core
    sibling = (gx + 1 - 2 * core, gz)

    def for_chips(act):
        def step(i, carry):
            xx, yy = (x + i // 4) % 4, (y + i % 4) % 4
            for dz in range(8):
                zz = (z + dz) % 8
                act(xx * 32 + yy * 8 + zz, ((xx % 2) * 64 + zz * 8 + yy * 2 + core, xx // 2))
            return carry

        for dz in range(1, 8):
            zz = (z + dz) % 8
            act(x * 32 + y * 8 + zz, (x_lo * 64 + zz * 8 + y * 2 + core, gz))
        lax.fori_loop(1, 16, step, 0)

    barrier = pltpu.get_barrier_semaphore()

    def signal(_, device):
        pl.semaphore_signal(barrier, inc=1, device_id=device, device_id_type=MESH)

    signal(0, sibling)
    for_chips(signal)

    def piece(a):
        return x_ref[:, a * 128 : (a + 1) * 128]

    fold[0] = piece(0)
    fold[8] = piece(8)
    for a in range(1, 8):
        first, second = piece(a), piece(16 - a)
        fold[a] = first + second
        fold[8 + a] = first - second

    def y_forward(group):
        if group < 7:
            c = group + 1
            real = fold[0] + (-1.0) ** c * fold[8]
            imag = None
            for a in range(1, 8):
                real = real + math.cos(2.0 * math.pi * a * c / 16) * fold[a]
                term = -math.sin(2.0 * math.pi * a * c / 16) * fold[8 + a]
                imag = term if imag is None else imag + term
            stacked = jnp.concatenate(
                [jnp.concatenate([real, -imag], axis=1), jnp.concatenate([imag, real], axis=1)], axis=0
            )
            table = (main_ref[0, group], main_ref[1, group])
        else:
            even = fold[0] + fold[8]
            for a in (2, 4, 6):
                even = even + fold[a]
            odd = fold[1]
            for a in (3, 5, 7):
                odd = odd + fold[a]
            pair = jnp.concatenate([even + odd, even - odd], axis=1)
            zero = jnp.zeros_like(pair)
            stacked = jnp.concatenate(
                [jnp.concatenate([pair, zero], axis=1), jnp.concatenate([zero, pair], axis=1)], axis=0
            )
            table = (packed_ref[0], packed_ref[1])
        high, low = split(stacked)
        yf[group] = dot_const_left(table, high, low, ((1,), (1,)))

    def groups_of(chunk):
        return [half * 4 + chunk * KEYS + t for half in range(2) for t in range(KEYS)]

    def core_copy(src, dst, chunk, send, recv):
        return pltpu.make_async_remote_copy(
            src_ref=src, dst_ref=dst, send_sem=send.at[chunk], recv_sem=recv.at[chunk],
            device_id=sibling, device_id_type=MESH,
        )

    def forward_core(chunk):
        return core_copy(yf.at[pl.ds(other * 4 + chunk * KEYS, KEYS)], sib_f.at[chunk], chunk, core_f_s, core_f_r)

    def chip_send(src, dst, chunk, send, recv):
        def go(chip, device):
            pltpu.make_async_remote_copy(
                src_ref=src.at[chunk, pl.ds(chip * ROWS, ROWS)],
                dst_ref=dst.at[chunk, pl.ds(me * ROWS, ROWS)],
                send_sem=send.at[chunk], recv_sem=recv.at[chunk],
                device_id=device, device_id_type=MESH,
            ).start()

        mine = pl.ds(me * ROWS, ROWS)
        pltpu.make_async_copy(src.at[chunk, mine], dst.at[chunk, mine], self_sem).start()
        for_chips(go)
        pltpu.make_async_copy(src.at[chunk, mine], dst.at[chunk, mine], self_sem).wait()

    def chip_wait(ref, chunk, sem):
        most = ref.at[chunk, pl.ds(0, 127 * ROWS)]
        pltpu.make_async_copy(most, most, sem.at[chunk]).wait()

    for group in groups_of(0):
        y_forward(group)
    pl.semaphore_wait(barrier, CHIPS)
    lane = lax.broadcasted_iota(jnp.int32, (8, 128), 1)
    row8 = lax.broadcasted_iota(jnp.int32, (8, 128), 0)
    upper = (lane // 16) % 2 == 1
    par[gz] = jnp.where(
        row8 < 4,
        jnp.where(upper, damp_ref[1], damp_ref[0]),
        jnp.where(upper, blend_ref[1], blend_ref[0]),
    )
    par_copy = pltpu.make_async_remote_copy(
        src_ref=par.at[gz], dst_ref=par.at[gz], send_sem=par_s, recv_sem=par_r,
        device_id=(gx, 1 - gz), device_id_type=MESH,
    )
    par_copy.start()

    def interleave(chunk):
        for t in range(KEYS):
            w1[chunk, pl.ds(t * 2 + core, CHIPS, stride=ROWS), :] = yf[core * 4 + chunk * KEYS + t]
            w1[chunk, pl.ds(t * 2 + other, CHIPS, stride=ROWS), :] = sib_f[chunk, t]

    forward_core(0).start()
    for chunk in range(CHUNKS):
        if chunk + 1 < CHUNKS:
            for group in groups_of(chunk + 1):
                y_forward(group)
        forward_core(chunk).wait_recv()
        if chunk + 1 < CHUNKS:
            forward_core(chunk + 1).start()
        interleave(chunk)
        chip_send(w1, r1, chunk, chip_f_s, chip_f_r)

    par_copy.wait()
    lane = lax.broadcasted_iota(jnp.int32, (128, 128), 1)
    mode = lax.broadcasted_iota(jnp.int32, (128, 128), 0) + 128 * (lane % 16)
    wave_x = jnp.where(mode < NX // 2, mode, mode - NX)
    wave_x = jnp.where(mode == NX // 2, 0, wave_x)
    along_x = (2.0 * math.pi / NX) * wave_x.astype(F32)
    second = (lane // 32) % 2 == 1
    for t in range(4):
        group = core * 4 + t
        slot = jnp.where(me < 64, me * 16, 8 + (me - 64) * 16)
        number = jnp.where(group == 7, slot, group + 1 + 16 * me)
        number = jnp.where(number < NY // 2, number, number - NY)
        once = jnp.logical_and(group == 7, me == 0)
        scale = jnp.where(once, 1.0, 2.0) * (1.0 / (NX * NY))
        along_y = jnp.full((128, 128), (2.0 * math.pi / NY) * number.astype(F32))
        squared = along_x * along_x + along_y * along_y
        anchor = squared == 0.0
        inverse = jnp.where(anchor, 0.0, 1.0 / jnp.where(anchor, 1.0, squared))
        cross = jnp.where(second, along_x, along_y)
        straight = jnp.where(anchor, 1.0, cross * cross * inverse) * scale
        mixed = -along_x * along_y * inverse * scale
        for half in range(2):
            damper = jnp.exp(-par[half, 0:1, :] * squared)
            coef[t, half, 0] = straight * damper
            coef[t, half, 1] = mixed * damper
    level_row = lax.broadcasted_iota(jnp.int32, (256, 256), 0)
    level_row = level_row // 128 * 2 + (level_row // 16) % 2
    weight = jnp.zeros((256, 256), F32)
    for level in range(4):
        value = jnp.max(par[level // 2, 4:5, (level % 2) * 16 : (level % 2) * 16 + 16])
        weight = jnp.where(level_row == level, value, weight)
    high, low = split(vert_ref[0] * weight + vert_ref[1] * (1.0 - weight))
    vmat[0] = high
    vmat[1] = low

    sign = jnp.where(lane < 64, 1.0, -1.0)

    def spun(value):
        return pltpu.roll(value, 64, axis=1)

    def doubled(first, second):
        top = jnp.concatenate([first, second], axis=1)
        bottom = jnp.concatenate([spun(first) * sign, spun(second) * sign], axis=1)
        return split(jnp.concatenate([top, bottom], axis=0))

    def column(chunk, local):
        t = chunk * KEYS + local
        even = r1[chunk, pl.ds(local * 2, CHIPS, stride=ROWS), :]
        odd = r1[chunk, pl.ds(local * 2 + 1, CHIPS, stride=ROWS), :]
        halves = [jnp.concatenate([even[h * 64 : h * 64 + 64], odd[h * 64 : h * 64 + 64]], axis=0) for h in range(2)]
        high, low = doubled(*halves)
        step = dot_const_left((slabf_ref[0], slabf_ref[1]), high, low)
        turned = []
        for h in range(2):
            part = step[:, h * 128 : h * 128 + 128]
            turned.append(part * twid_ref[0] + spun(part) * twid_ref[1])
        high, low = split(jnp.concatenate(turned, axis=0))
        modes = dot_const_right(high, low, (mix_ref[0], mix_ref[1]))
        kept = []
        for h in range(2):
            rows = slice(h * 128, h * 128 + 128)
            kept.append(modes[rows, :128] * coef[t, h, 0] + modes[rows, 128:] * coef[t, h, 1])
        high, low = split(jnp.concatenate(kept, axis=1))
        back = dot_const_right(high, low, (vmat[0], vmat[1]))
        turned = []
        for h in range(2):
            part = back[:, h * 128 : h * 128 + 128]
            turned.append(part * twid_ref[0] - spun(part) * twid_ref[1])
        high, low = doubled(*turned)
        result = dot_const_left((slabi_ref[0], slabi_ref[1]), high, low)
        for h in range(2):
            for c in range(2):
                w2[chunk, pl.ds(h * 64 * ROWS + local * 2 + c, 64, stride=ROWS), :] = result[
                    c * 64 : c * 64 + 64, h * 128 : h * 128 + 128
                ]

    for chunk in range(CHUNKS):
        chip_wait(r1, chunk, chip_f_r)
        for local in range(KEYS):
            column(chunk, local)
        chip_send(w2, r2, chunk, chip_b_s, chip_b_r)

    def backward_core(chunk):
        return core_copy(own_b.at[chunk], yb.at[pl.ds(core * 4 + chunk * KEYS, KEYS)], chunk, core_b_s, core_b_r)

    def y_backward(group):
        data = yb[group].T
        high, low = split(data)
        if group < 7:
            c = group + 1
            full = dot_const_right(high, low, (main_ref[0, group], main_ref[1, group]))
            real = full[:64, :128] + full[64:, 128:]
            imag = full[64:, :128] - full[:64, 128:]
            for a in range(9):
                factor = math.cos(2.0 * math.pi * a * c / 16)
                acc_e[a] = factor * real if group == 0 else acc_e[a] + factor * real
            for a in range(1, 8):
                factor = math.sin(2.0 * math.pi * a * c / 16)
                acc_o[a] = factor * imag if group == 0 else acc_o[a] + factor * imag
        else:
            both = dot_const_right(high[:64], low[:64], (packed_ref[0, :, :256], packed_ref[1, :, :256]))
            both = both + dot_const_right(high[64:], low[64:], (packed_ref[0, :, 256:], packed_ref[1, :, 256:]))
            for a in range(9):
                acc_e[a] = acc_e[a] + (both[:, :128] + (-1.0) ** a * both[:, 128:])

    for chunk in range(CHUNKS):
        chip_wait(r2, chunk, chip_b_r)
        for t in range(KEYS):
            own_b[chunk, t] = r2[chunk, pl.ds(t * 2 + other, CHIPS, stride=ROWS), :]
        backward_core(chunk).start()
        for t in range(KEYS):
            yb[core * 4 + chunk * KEYS + t] = r2[chunk, pl.ds(t * 2 + core, CHIPS, stride=ROWS), :]
        backward_core(chunk).wait_recv()
        for group in groups_of(chunk):
            y_backward(group)

    out_ref[:, 0:128] = acc_e[0]
    out_ref[:, 1024:1152] = acc_e[8]
    for a in range(1, 8):
        out_ref[:, a * 128 : a * 128 + 128] = acc_e[a] - acc_o[a]
        out_ref[:, (16 - a) * 128 : (16 - a) * 128 + 128] = acc_e[a] + acc_o[a]

    for chunk in range(CHUNKS):
        forward_core(chunk).wait_send()
        backward_core(chunk).wait_send()
        chip_wait(w1, chunk, chip_f_s)
        chip_wait(w2, chunk, chip_b_s)


def body(cotangent, damping, blending):
    consts = [jnp.asarray(table) for table in tables()]
    vmem = pl.BlockSpec(memory_space=pltpu.VMEM)
    smem = pl.BlockSpec(memory_space=pltpu.SMEM)
    dma = pltpu.SemaphoreType.DMA
    scratch = [
        ((16, 64, 128), F32),
        ((8, 128, 128), F32),
        ((CHUNKS, KEYS, 128, 128), F32),
        ((CHUNKS, CHIPS * ROWS, 128), F32),
        ((CHUNKS, CHIPS * ROWS, 128), F32),
        ((4, 2, 2, 128, 128), F32),
        ((2, 256, 256), BF16),
        ((CHUNKS, CHIPS * ROWS, 128), F32),
        ((CHUNKS, CHIPS * ROWS, 128), F32),
        ((CHUNKS, KEYS, 128, 128), F32),
        ((8, 128, 128), F32),
        ((9, 64, 128), F32),
        ((8, 64, 128), F32),
        ((2, 8, 128), F32),
    ]
    result = pl.pallas_call(
        kernel,
        out_shape=jax.ShapeDtypeStruct((64, NY), F32),
        in_specs=[vmem, smem, smem] + [vmem] * len(consts),
        out_specs=vmem,
        scratch_shapes=[pltpu.VMEM(*s) for s in scratch] + [dma((CHUNKS,))] * 8 + [dma, dma, dma],
        compiler_params=pltpu.CompilerParams(
            collective_id=0, has_side_effects=True, vmem_limit_bytes=48 * 1024 * 1024
        ),
    )(cotangent.reshape(64, NY), damping, blending, *consts)
    return result.reshape(2, 2, 16, NY)


def solution(mesh):
    return jax.shard_map(
        body,
        mesh=mesh,
        in_specs=(P(None, "gz", "gx", None), P("gz"), P("gz")),
        out_specs=P(None, "gz", "gx", None),
        check_vma=False,
    )
```

```python
import functools
import math

import jax
import jax.numpy as jnp
import numpy as np
from jax import lax
from jax.experimental import pallas as pl
from jax.experimental.pallas import tpu as pltpu
from jax.sharding import PartitionSpec as P

NX = 2048
NY = 2048
CHIPS = 128
LANES = 128
GROUPS = 8
CHUNKS = 2
KEYS = 4 // CHUNKS
ROWS = 2 * KEYS
MESH = pl.DeviceIdType.MESH
F32 = jnp.float32
BF16 = jnp.bfloat16


def split_const(table):
    table = np.asarray(table, np.float32)
    high = table.astype(BF16)
    low = (table - high.astype(np.float32)).astype(BF16)
    return np.stack([high, low])


def wave(numerator, period):
    angle = 2.0 * np.pi * (np.asarray(numerator, np.int64) % period) / period
    return np.cos(angle), np.sin(angle)


@functools.cache
def tables():
    d = np.arange(128)[:, None]
    b = np.arange(128)[None, :]
    groups = []
    for c in range(1, 8):
        cos, sin = wave(b * (c + 16 * d), NY)
        groups.append(np.concatenate([cos, -sin], axis=1))
    main = split_const(np.stack(groups))
    half = np.arange(64)[:, None]
    cos0, sin0 = wave(b * (16 * half), NY)
    cos8, sin8 = wave(b * (8 + 16 * half), NY)
    im0 = -sin0
    im0[0] = 1.0 - 2.0 * (np.arange(128) % 2)
    zero = np.zeros((64, 128))
    packed = np.block([[cos0, zero, im0, zero], [zero, cos8, zero, -sin8]])
    packed = split_const(packed)
    core, x_lo, y, z = np.meshgrid(range(2), range(2), range(4), range(8), indexing="ij")
    slab = (x_lo * 64 + z * 8 + y * 2 + core).reshape(-1)
    k1 = np.arange(128)
    cos, sin = wave(k1[:, None] * slab[None, :], 128)
    slab_fwd = split_const(np.concatenate([cos, sin], axis=1))
    slab_inv = split_const(np.concatenate([cos.T, -sin.T], axis=1))
    lane = np.arange(128)
    cos, sin = wave(k1[:, None] * (lane % 16)[None, :], NX)
    sign = np.where(lane < 64, 1.0, -1.0)[None, :]
    twiddle = np.stack([cos, sin * sign]).astype(np.float32)
    src, dst = lane[:, None], lane[None, :]
    same = (src // 16) % 4 == (dst // 16) % 4
    cos, sin = wave((src % 16) * (dst % 16), 16)
    src_im, dst_im = src // 64, dst // 64
    fwd = np.where(src_im == dst_im, cos, np.where(dst_im == 0, sin, -sin)) * same
    inv = np.where(src_im == dst_im, cos, np.where(dst_im == 0, -sin, sin))
    mix = split_const(np.concatenate([fwd, fwd[:, lane ^ 32]], axis=1))
    row = np.arange(256)[:, None]
    col = np.arange(256)[None, :]
    level_row = (row // 128) * 2 + (row // 16) % 2
    level_col = (col // 128) * 2 + (col // 16) % 2
    same_c = (row // 32) % 2 == (col // 32) % 2
    inv = np.tile(inv, (2, 2)) * same_c
    keep = inv * (level_row == level_col)
    carry = inv * (level_row + 1 == level_col)
    vertical = np.stack([keep, carry]).astype(np.float32)
    return main, packed, slab_fwd, slab_inv, twiddle, mix, vertical


def split(value):
    high = value.astype(BF16)
    low = (value - high.astype(F32)).astype(BF16)
    return high, low


def dot(a, b, dims):
    return lax.dot_general(a, b, (dims, ((), ())), preferred_element_type=F32)


def dot_const_left(table, high, low, dims=((1,), (0,))):
    c_high, c_low = table
    return dot(c_high, high, dims) + (dot(c_low, high, dims) + dot(c_high, low, dims))


def dot_const_right(high, low, table, dims=((1,), (0,))):
    c_high, c_low = table
    return dot(high, c_high, dims) + (dot(low, c_high, dims) + dot(high, c_low, dims))


def kernel(
    x_hbm, damp_hbm, blend_hbm, main_hbm, packed_hbm, slabf_hbm, slabi_hbm, twid_hbm, mix_hbm, vert_hbm,
    out_ref,
    x_ref, damp_ref, blend_ref, main_ref, packed_ref, slabf_ref, slabi_ref, twid_ref, mix_ref, vert_ref,
    fold, yf, sib_f, w1, r1, coef, vmat, w2, r2, own_b, yb, acc_e, acc_o, par,
    core_f_s, core_f_r, chip_f_s, chip_f_r, chip_b_s, chip_b_r, core_b_s, core_b_r, par_s, par_r, self_sem, load_sem,
):
    gx = lax.axis_index("gx")
    gz = lax.axis_index("gz")
    x_lo, z, y, core = gx // 64, (gx // 8) % 8, (gx // 2) % 4, gx % 2
    x = gz * 2 + x_lo
    me = x * 32 + y * 8 + z
    other = 1 - core
    sibling = (gx + 1 - 2 * core, gz)

    def for_chips(act):
        def step(i, carry):
            xx, yy = (x + i // 4) % 4, (y + i % 4) % 4
            for dz in range(8):
                zz = (z + dz) % 8
                act(xx * 32 + yy * 8 + zz, ((xx % 2) * 64 + zz * 8 + yy * 2 + core, xx // 2))
            return carry

        for dz in range(1, 8):
            zz = (z + dz) % 8
            act(x * 32 + y * 8 + zz, (x_lo * 64 + zz * 8 + y * 2 + core, gz))
        lax.fori_loop(1, 16, step, 0)

    sources = [x_hbm, main_hbm, packed_hbm, damp_hbm, blend_hbm, slabf_hbm, twid_hbm, mix_hbm, vert_hbm, slabi_hbm]
    targets = [x_ref, main_ref, packed_ref, damp_ref, blend_ref, slabf_ref, twid_ref, mix_ref, vert_ref, slabi_ref]
    loads = [pltpu.make_async_copy(s, t, load_sem.at[i]) for i, (s, t) in enumerate(zip(sources, targets))]
    for load in loads:
        load.start()
    barrier = pltpu.get_barrier_semaphore()

    def signal(_, device):
        pl.semaphore_signal(barrier, inc=1, device_id=device, device_id_type=MESH)

    signal(0, sibling)
    for_chips(signal)

    for load in loads[:3]:
        load.wait()

    def piece(a):
        return x_ref[:, a * 128 : (a + 1) * 128]

    fold[0] = piece(0)
    fold[8] = piece(8)
    for a in range(1, 8):
        first, second = piece(a), piece(16 - a)
        fold[a] = first + second
        fold[8 + a] = first - second

    def y_forward(group):
        if group < 7:
            c = group + 1
            real = fold[0] + (-1.0) ** c * fold[8]
            imag = None
            for a in range(1, 8):
                real = real + math.cos(2.0 * math.pi * a * c / 16) * fold[a]
                term = -math.sin(2.0 * math.pi * a * c / 16) * fold[8 + a]
                imag = term if imag is None else imag + term
            stacked = jnp.concatenate(
                [jnp.concatenate([real, -imag], axis=1), jnp.concatenate([imag, real], axis=1)], axis=0
            )
            table = (main_ref[0, group], main_ref[1, group])
        else:
            even = fold[0] + fold[8]
            for a in (2, 4, 6):
                even = even + fold[a]
            odd = fold[1]
            for a in (3, 5, 7):
                odd = odd + fold[a]
            pair = jnp.concatenate([even + odd, even - odd], axis=1)
            zero = jnp.zeros_like(pair)
            stacked = jnp.concatenate(
                [jnp.concatenate([pair, zero], axis=1), jnp.concatenate([zero, pair], axis=1)], axis=0
            )
            table = (packed_ref[0], packed_ref[1])
        high, low = split(stacked)
        yf[group] = dot_const_left(table, high, low, ((1,), (1,)))

    def groups_of(chunk):
        return [half * 4 + chunk * KEYS + t for half in range(2) for t in range(KEYS)]

    def core_copy(src, dst, chunk, send, recv):
        return pltpu.make_async_remote_copy(
            src_ref=src, dst_ref=dst, send_sem=send.at[chunk], recv_sem=recv.at[chunk],
            device_id=sibling, device_id_type=MESH,
        )

    def forward_core(chunk):
        return core_copy(yf.at[pl.ds(other * 4 + chunk * KEYS, KEYS)], sib_f.at[chunk], chunk, core_f_s, core_f_r)

    def chip_send(src, dst, chunk, send, recv):
        def go(chip, device):
            pltpu.make_async_remote_copy(
                src_ref=src.at[chunk, pl.ds(chip * ROWS, ROWS)],
                dst_ref=dst.at[chunk, pl.ds(me * ROWS, ROWS)],
                send_sem=send.at[chunk], recv_sem=recv.at[chunk],
                device_id=device, device_id_type=MESH,
            ).start()

        mine = pl.ds(me * ROWS, ROWS)
        pltpu.make_async_copy(src.at[chunk, mine], dst.at[chunk, mine], self_sem).start()
        for_chips(go)
        pltpu.make_async_copy(src.at[chunk, mine], dst.at[chunk, mine], self_sem).wait()

    def chip_wait(ref, chunk, sem):
        most = ref.at[chunk, pl.ds(0, 127 * ROWS)]
        pltpu.make_async_copy(most, most, sem.at[chunk]).wait()

    for group in groups_of(0):
        y_forward(group)
    pl.semaphore_wait(barrier, CHIPS)
    for load in loads[3:]:
        load.wait()
    lane = lax.broadcasted_iota(jnp.int32, (8, 128), 1)
    row8 = lax.broadcasted_iota(jnp.int32, (8, 128), 0)
    upper = (lane // 16) % 2 == 1
    par[gz] = jnp.where(
        row8 < 4,
        jnp.where(upper, damp_ref[1], damp_ref[0]),
        jnp.where(upper, blend_ref[1], blend_ref[0]),
    )
    par_copy = pltpu.make_async_remote_copy(
        src_ref=par.at[gz], dst_ref=par.at[gz], send_sem=par_s, recv_sem=par_r,
        device_id=(gx, 1 - gz), device_id_type=MESH,
    )
    par_copy.start()

    def interleave(chunk):
        for t in range(KEYS):
            w1[chunk, pl.ds(t * 2 + core, CHIPS, stride=ROWS), :] = yf[core * 4 + chunk * KEYS + t]
            w1[chunk, pl.ds(t * 2 + other, CHIPS, stride=ROWS), :] = sib_f[chunk, t]

    forward_core(0).start()
    for chunk in range(CHUNKS):
        if chunk + 1 < CHUNKS:
            for group in groups_of(chunk + 1):
                y_forward(group)
        forward_core(chunk).wait_recv()
        if chunk + 1 < CHUNKS:
            forward_core(chunk + 1).start()
        interleave(chunk)
        chip_send(w1, r1, chunk, chip_f_s, chip_f_r)

    par_copy.wait()
    lane = lax.broadcasted_iota(jnp.int32, (128, 128), 1)
    mode = lax.broadcasted_iota(jnp.int32, (128, 128), 0) + 128 * (lane % 16)
    wave_x = jnp.where(mode < NX // 2, mode, mode - NX)
    wave_x = jnp.where(mode == NX // 2, 0, wave_x)
    along_x = (2.0 * math.pi / NX) * wave_x.astype(F32)
    second = (lane // 32) % 2 == 1
    for t in range(4):
        group = core * 4 + t
        slot = jnp.where(me < 64, me * 16, 8 + (me - 64) * 16)
        number = jnp.where(group == 7, slot, group + 1 + 16 * me)
        number = jnp.where(number < NY // 2, number, number - NY)
        once = jnp.logical_and(group == 7, me == 0)
        scale = jnp.where(once, 1.0, 2.0) * (1.0 / (NX * NY))
        along_y = jnp.full((128, 128), (2.0 * math.pi / NY) * number.astype(F32))
        squared = along_x * along_x + along_y * along_y
        anchor = squared == 0.0
        inverse = jnp.where(anchor, 0.0, 1.0 / jnp.where(anchor, 1.0, squared))
        cross = jnp.where(second, along_x, along_y)
        straight = jnp.where(anchor, 1.0, cross * cross * inverse) * scale
        mixed = -along_x * along_y * inverse * scale
        for half in range(2):
            damper = jnp.exp(-par[half, 0:1, :] * squared)
            coef[t, half, 0] = straight * damper
            coef[t, half, 1] = mixed * damper
    level_row = lax.broadcasted_iota(jnp.int32, (256, 256), 0)
    level_row = level_row // 128 * 2 + (level_row // 16) % 2
    weight = jnp.zeros((256, 256), F32)
    for level in range(4):
        value = jnp.max(par[level // 2, 4:5, (level % 2) * 16 : (level % 2) * 16 + 16])
        weight = jnp.where(level_row == level, value, weight)
    high, low = split(vert_ref[0] * weight + vert_ref[1] * (1.0 - weight))
    vmat[0] = high
    vmat[1] = low

    sign = jnp.where(lane < 64, 1.0, -1.0)

    def spun(value):
        return pltpu.roll(value, 64, axis=1)

    def doubled(first, second):
        top = jnp.concatenate([first, second], axis=1)
        bottom = jnp.concatenate([spun(first) * sign, spun(second) * sign], axis=1)
        return split(jnp.concatenate([top, bottom], axis=0))

    def column(chunk, local):
        t = chunk * KEYS + local
        even = r1[chunk, pl.ds(local * 2, CHIPS, stride=ROWS), :]
        odd = r1[chunk, pl.ds(local * 2 + 1, CHIPS, stride=ROWS), :]
        halves = [jnp.concatenate([even[h * 64 : h * 64 + 64], odd[h * 64 : h * 64 + 64]], axis=0) for h in range(2)]
        high, low = doubled(*halves)
        step = dot_const_left((slabf_ref[0], slabf_ref[1]), high, low)
        turned = []
        for h in range(2):
            part = step[:, h * 128 : h * 128 + 128]
            turned.append(part * twid_ref[0] + spun(part) * twid_ref[1])
        high, low = split(jnp.concatenate(turned, axis=0))
        modes = dot_const_right(high, low, (mix_ref[0], mix_ref[1]))
        kept = []
        for h in range(2):
            rows = slice(h * 128, h * 128 + 128)
            kept.append(modes[rows, :128] * coef[t, h, 0] + modes[rows, 128:] * coef[t, h, 1])
        high, low = split(jnp.concatenate(kept, axis=1))
        back = dot_const_right(high, low, (vmat[0], vmat[1]))
        turned = []
        for h in range(2):
            part = back[:, h * 128 : h * 128 + 128]
            turned.append(part * twid_ref[0] - spun(part) * twid_ref[1])
        high, low = doubled(*turned)
        result = dot_const_left((slabi_ref[0], slabi_ref[1]), high, low)
        for h in range(2):
            for c in range(2):
                w2[chunk, pl.ds(h * 64 * ROWS + local * 2 + c, 64, stride=ROWS), :] = result[
                    c * 64 : c * 64 + 64, h * 128 : h * 128 + 128
                ]

    for chunk in range(CHUNKS):
        chip_wait(r1, chunk, chip_f_r)
        for local in range(KEYS):
            column(chunk, local)
        chip_send(w2, r2, chunk, chip_b_s, chip_b_r)

    def backward_core(chunk):
        return core_copy(own_b.at[chunk], yb.at[pl.ds(core * 4 + chunk * KEYS, KEYS)], chunk, core_b_s, core_b_r)

    def y_backward(group):
        data = yb[group].T
        high, low = split(data)
        if group < 7:
            c = group + 1
            full = dot_const_right(high, low, (main_ref[0, group], main_ref[1, group]))
            real = full[:64, :128] + full[64:, 128:]
            imag = full[64:, :128] - full[:64, 128:]
            for a in range(9):
                factor = math.cos(2.0 * math.pi * a * c / 16)
                acc_e[a] = factor * real if group == 0 else acc_e[a] + factor * real
            for a in range(1, 8):
                factor = math.sin(2.0 * math.pi * a * c / 16)
                acc_o[a] = factor * imag if group == 0 else acc_o[a] + factor * imag
        else:
            both = dot_const_right(high[:64], low[:64], (packed_ref[0, :, :256], packed_ref[1, :, :256]))
            both = both + dot_const_right(high[64:], low[64:], (packed_ref[0, :, 256:], packed_ref[1, :, 256:]))
            for a in range(9):
                acc_e[a] = acc_e[a] + (both[:, :128] + (-1.0) ** a * both[:, 128:])

    for chunk in range(CHUNKS):
        chip_wait(r2, chunk, chip_b_r)
        for t in range(KEYS):
            own_b[chunk, t] = r2[chunk, pl.ds(t * 2 + other, CHIPS, stride=ROWS), :]
        backward_core(chunk).start()
        for t in range(KEYS):
            yb[core * 4 + chunk * KEYS + t] = r2[chunk, pl.ds(t * 2 + core, CHIPS, stride=ROWS), :]
        backward_core(chunk).wait_recv()
        for group in groups_of(chunk):
            y_backward(group)

    out_ref[:, 0:128] = acc_e[0]
    out_ref[:, 1024:1152] = acc_e[8]
    for a in range(1, 8):
        out_ref[:, a * 128 : a * 128 + 128] = acc_e[a] - acc_o[a]
        out_ref[:, (16 - a) * 128 : (16 - a) * 128 + 128] = acc_e[a] + acc_o[a]

    for chunk in range(CHUNKS):
        forward_core(chunk).wait_send()
        backward_core(chunk).wait_send()
        chip_wait(w1, chunk, chip_f_s)
        chip_wait(w2, chunk, chip_b_s)


def body(cotangent, damping, blending):
    consts = [jnp.asarray(table) for table in tables()]
    anywhere = pl.BlockSpec(memory_space=pltpu.HBM)
    dma = pltpu.SemaphoreType.DMA
    scratch = [
        ((16, 64, 128), F32),
        ((8, 128, 128), F32),
        ((CHUNKS, KEYS, 128, 128), F32),
        ((CHUNKS, CHIPS * ROWS, 128), F32),
        ((CHUNKS, CHIPS * ROWS, 128), F32),
        ((4, 2, 2, 128, 128), F32),
        ((2, 256, 256), BF16),
        ((CHUNKS, CHIPS * ROWS, 128), F32),
        ((CHUNKS, CHIPS * ROWS, 128), F32),
        ((CHUNKS, KEYS, 128, 128), F32),
        ((8, 128, 128), F32),
        ((9, 64, 128), F32),
        ((8, 64, 128), F32),
        ((2, 8, 128), F32),
    ]
    result = pl.pallas_call(
        kernel,
        out_shape=jax.ShapeDtypeStruct((64, NY), F32),
        in_specs=[anywhere] * (3 + len(consts)),
        out_specs=pl.BlockSpec(memory_space=pltpu.VMEM),
        scratch_shapes=[pltpu.VMEM((64, NY), F32), pltpu.SMEM((2,), F32), pltpu.SMEM((2,), F32)]
        + [pltpu.VMEM(c.shape, c.dtype) for c in consts]
        + [pltpu.VMEM(*s) for s in scratch]
        + [dma((CHUNKS,))] * 8
        + [dma, dma, dma, dma((3 + len(consts),))],
        compiler_params=pltpu.CompilerParams(
            collective_id=0, has_side_effects=True, vmem_limit_bytes=62 * 1024 * 1024
        ),
    )(cotangent.reshape(64, NY), damping, blending, *consts)
    return result.reshape(2, 2, 16, NY)


def solution(mesh):
    return jax.shard_map(
        body,
        mesh=mesh,
        in_specs=(P(None, "gz", "gx", None), P("gz"), P("gz")),
        out_specs=P(None, "gz", "gx", None),
        check_vma=False,
    )
```

```python
import functools
import math

import jax
import jax.numpy as jnp
import numpy as np
from jax import lax
from jax.experimental import pallas as pl
from jax.experimental.pallas import tpu as pltpu
from jax.sharding import PartitionSpec as P

NX = 2048
NY = 2048
CHIPS = 128
LANES = 128
GROUPS = 8
CHUNKS = 4
KEYS = 4 // CHUNKS
ROWS = 2 * KEYS
MESH = pl.DeviceIdType.MESH
F32 = jnp.float32
BF16 = jnp.bfloat16


def split_const(table):
    table = np.asarray(table, np.float32)
    high = table.astype(BF16)
    low = (table - high.astype(np.float32)).astype(BF16)
    return np.stack([high, low])


def wave(numerator, period):
    angle = 2.0 * np.pi * (np.asarray(numerator, np.int64) % period) / period
    return np.cos(angle), np.sin(angle)


@functools.cache
def tables():
    d = np.arange(128)[:, None]
    b = np.arange(128)[None, :]
    groups = []
    for c in range(1, 8):
        cos, sin = wave(b * (c + 16 * d), NY)
        groups.append(np.concatenate([cos, -sin], axis=1))
    main = split_const(np.stack(groups))
    half = np.arange(64)[:, None]
    cos0, sin0 = wave(b * (16 * half), NY)
    cos8, sin8 = wave(b * (8 + 16 * half), NY)
    im0 = -sin0
    im0[0] = 1.0 - 2.0 * (np.arange(128) % 2)
    zero = np.zeros((64, 128))
    packed = np.block([[cos0, zero, im0, zero], [zero, cos8, zero, -sin8]])
    packed = split_const(packed)
    core, x_lo, y, z = np.meshgrid(range(2), range(2), range(4), range(8), indexing="ij")
    slab = (x_lo * 64 + z * 8 + y * 2 + core).reshape(-1)
    k1 = np.arange(128)
    cos, sin = wave(k1[:, None] * slab[None, :], 128)
    slab_fwd = split_const(np.concatenate([cos, sin], axis=1))
    slab_inv = split_const(np.concatenate([cos.T, -sin.T], axis=1))
    lane = np.arange(128)
    cos, sin = wave(k1[:, None] * (lane % 16)[None, :], NX)
    sign = np.where(lane < 64, 1.0, -1.0)[None, :]
    twiddle = np.stack([cos, sin * sign]).astype(np.float32)
    src, dst = lane[:, None], lane[None, :]
    same = (src // 16) % 4 == (dst // 16) % 4
    cos, sin = wave((src % 16) * (dst % 16), 16)
    src_im, dst_im = src // 64, dst // 64
    fwd = np.where(src_im == dst_im, cos, np.where(dst_im == 0, sin, -sin)) * same
    inv = np.where(src_im == dst_im, cos, np.where(dst_im == 0, -sin, sin))
    mix = split_const(np.concatenate([fwd, fwd[:, lane ^ 32]], axis=1))
    row = np.arange(256)[:, None]
    col = np.arange(256)[None, :]
    level_row = (row // 128) * 2 + (row // 16) % 2
    level_col = (col // 128) * 2 + (col // 16) % 2
    same_c = (row // 32) % 2 == (col // 32) % 2
    inv = np.tile(inv, (2, 2)) * same_c
    keep = inv * (level_row == level_col)
    carry = inv * (level_row + 1 == level_col)
    vertical = np.stack([keep, carry]).astype(np.float32)
    return main, packed, slab_fwd, slab_inv, twiddle, mix, vertical


def split(value):
    high = value.astype(BF16)
    low = (value - high.astype(F32)).astype(BF16)
    return high, low


def dot(a, b, dims):
    return lax.dot_general(a, b, (dims, ((), ())), preferred_element_type=F32)


def dot_const_left(table, high, low, dims=((1,), (0,))):
    c_high, c_low = table
    return dot(c_high, high, dims) + (dot(c_low, high, dims) + dot(c_high, low, dims))


def dot_const_right(high, low, table, dims=((1,), (0,))):
    c_high, c_low = table
    return dot(high, c_high, dims) + (dot(low, c_high, dims) + dot(high, c_low, dims))


def kernel(
    x_hbm, damp_hbm, blend_hbm, main_hbm, packed_hbm, slabf_hbm, slabi_hbm, twid_hbm, mix_hbm, vert_hbm,
    out_ref,
    x_ref, damp_ref, blend_ref, main_ref, packed_ref, slabf_ref, slabi_ref, twid_ref, mix_ref, vert_ref,
    fold, yf, sib_f, w1, r1, coef, vmat, w2, r2, own_b, yb, acc_e, acc_o, par,
    core_f_s, core_f_r, chip_f_s, chip_f_r, chip_b_s, chip_b_r, core_b_s, core_b_r, par_s, par_r, self_sem, load_sem,
):
    gx = lax.axis_index("gx")
    gz = lax.axis_index("gz")
    x_lo, z, y, core = gx // 64, (gx // 8) % 8, (gx // 2) % 4, gx % 2
    x = gz * 2 + x_lo
    me = x * 32 + y * 8 + z
    other = 1 - core
    sibling = (gx + 1 - 2 * core, gz)

    def for_chips(act):
        xs = [(x + dx) % 4 for dx in range(4)]
        ys = [(y + dy) % 4 for dy in range(4)]
        zs = [(z + dz) % 8 for dz in range(8)]
        for dx in (2, 1, 3, 0):
            for dy in (2, 1, 3, 0):
                base = xs[dx] * 32 + ys[dy] * 8
                gbase = (xs[dx] % 2) * 64 + ys[dy] * 2 + core
                for dz in (4, 3, 5, 2, 6, 1, 7, 0):
                    if dx or dy or dz:
                        act(base + zs[dz], (gbase + zs[dz] * 8, xs[dx] // 2))

    sources = [x_hbm, main_hbm, packed_hbm, damp_hbm, blend_hbm, slabf_hbm, twid_hbm, mix_hbm, vert_hbm, slabi_hbm]
    targets = [x_ref, main_ref, packed_ref, damp_ref, blend_ref, slabf_ref, twid_ref, mix_ref, vert_ref, slabi_ref]
    loads = [pltpu.make_async_copy(s, t, load_sem.at[i]) for i, (s, t) in enumerate(zip(sources, targets))]
    for load in loads:
        load.start()
    barrier = pltpu.get_barrier_semaphore()

    def signal(_, device):
        pl.semaphore_signal(barrier, inc=1, device_id=device, device_id_type=MESH)

    signal(0, sibling)
    for_chips(signal)

    for load in loads[:3]:
        load.wait()

    def piece(a):
        return x_ref[:, a * 128 : (a + 1) * 128]

    fold[0] = piece(0)
    fold[8] = piece(8)
    for a in range(1, 8):
        first, second = piece(a), piece(16 - a)
        fold[a] = first + second
        fold[8 + a] = first - second

    def y_forward(group):
        if group < 7:
            c = group + 1
            real = fold[0] + (-1.0) ** c * fold[8]
            imag = None
            for a in range(1, 8):
                real = real + math.cos(2.0 * math.pi * a * c / 16) * fold[a]
                term = -math.sin(2.0 * math.pi * a * c / 16) * fold[8 + a]
                imag = term if imag is None else imag + term
            stacked = jnp.concatenate(
                [jnp.concatenate([real, -imag], axis=1), jnp.concatenate([imag, real], axis=1)], axis=0
            )
            table = (main_ref[0, group], main_ref[1, group])
        else:
            even = fold[0] + fold[8]
            for a in (2, 4, 6):
                even = even + fold[a]
            odd = fold[1]
            for a in (3, 5, 7):
                odd = odd + fold[a]
            pair = jnp.concatenate([even + odd, even - odd], axis=1)
            zero = jnp.zeros_like(pair)
            stacked = jnp.concatenate(
                [jnp.concatenate([pair, zero], axis=1), jnp.concatenate([zero, pair], axis=1)], axis=0
            )
            table = (packed_ref[0], packed_ref[1])
        high, low = split(stacked)
        yf[group] = dot_const_left(table, high, low, ((1,), (1,)))

    def groups_of(chunk):
        return [half * 4 + chunk * KEYS + t for half in range(2) for t in range(KEYS)]

    def core_copy(src, dst, chunk, send, recv):
        return pltpu.make_async_remote_copy(
            src_ref=src, dst_ref=dst, send_sem=send.at[chunk], recv_sem=recv.at[chunk],
            device_id=sibling, device_id_type=MESH,
        )

    def forward_core(chunk):
        return core_copy(yf.at[pl.ds(other * 4 + chunk * KEYS, KEYS)], sib_f.at[chunk], chunk, core_f_s, core_f_r)

    def chip_send(src, dst, chunk, send, recv):
        def go(chip, device):
            pltpu.make_async_remote_copy(
                src_ref=src.at[chunk, pl.ds(chip * ROWS, ROWS)],
                dst_ref=dst.at[chunk, pl.ds(me * ROWS, ROWS)],
                send_sem=send.at[chunk], recv_sem=recv.at[chunk],
                device_id=device, device_id_type=MESH,
            ).start()

        mine = pl.ds(me * ROWS, ROWS)
        pltpu.make_async_copy(src.at[chunk, mine], dst.at[chunk, mine], self_sem).start()
        for_chips(go)
        pltpu.make_async_copy(src.at[chunk, mine], dst.at[chunk, mine], self_sem).wait()

    def chip_wait(ref, chunk, sem):
        most = ref.at[chunk, pl.ds(0, 127 * ROWS)]
        pltpu.make_async_copy(most, most, sem.at[chunk]).wait()

    for group in groups_of(0):
        y_forward(group)
    pl.semaphore_wait(barrier, CHIPS)
    for load in loads[3:]:
        load.wait()
    lane = lax.broadcasted_iota(jnp.int32, (8, 128), 1)
    row8 = lax.broadcasted_iota(jnp.int32, (8, 128), 0)
    upper = (lane // 16) % 2 == 1
    par[gz] = jnp.where(
        row8 < 4,
        jnp.where(upper, damp_ref[1], damp_ref[0]),
        jnp.where(upper, blend_ref[1], blend_ref[0]),
    )
    par_copy = pltpu.make_async_remote_copy(
        src_ref=par.at[gz], dst_ref=par.at[gz], send_sem=par_s, recv_sem=par_r,
        device_id=(gx, 1 - gz), device_id_type=MESH,
    )
    par_copy.start()

    def interleave(chunk):
        for t in range(KEYS):
            w1[chunk, pl.ds(t * 2 + core, CHIPS, stride=ROWS), :] = yf[core * 4 + chunk * KEYS + t]
            w1[chunk, pl.ds(t * 2 + other, CHIPS, stride=ROWS), :] = sib_f[chunk, t]

    forward_core(0).start()
    for chunk in range(CHUNKS):
        if chunk + 1 < CHUNKS:
            for group in groups_of(chunk + 1):
                y_forward(group)
        forward_core(chunk).wait_recv()
        if chunk + 1 < CHUNKS:
            forward_core(chunk + 1).start()
        interleave(chunk)
        chip_send(w1, r1, chunk, chip_f_s, chip_f_r)

    par_copy.wait()
    lane = lax.broadcasted_iota(jnp.int32, (128, 128), 1)
    mode = lax.broadcasted_iota(jnp.int32, (128, 128), 0) + 128 * (lane % 16)
    wave_x = jnp.where(mode < NX // 2, mode, mode - NX)
    wave_x = jnp.where(mode == NX // 2, 0, wave_x)
    along_x = (2.0 * math.pi / NX) * wave_x.astype(F32)
    second = (lane // 32) % 2 == 1
    for t in range(4):
        group = core * 4 + t
        slot = jnp.where(me < 64, me * 16, 8 + (me - 64) * 16)
        number = jnp.where(group == 7, slot, group + 1 + 16 * me)
        number = jnp.where(number < NY // 2, number, number - NY)
        once = jnp.logical_and(group == 7, me == 0)
        scale = jnp.where(once, 1.0, 2.0) * (1.0 / (NX * NY))
        along_y = jnp.full((128, 128), (2.0 * math.pi / NY) * number.astype(F32))
        squared = along_x * along_x + along_y * along_y
        anchor = squared == 0.0
        inverse = jnp.where(anchor, 0.0, 1.0 / jnp.where(anchor, 1.0, squared))
        cross = jnp.where(second, along_x, along_y)
        straight = jnp.where(anchor, 1.0, cross * cross * inverse) * scale
        mixed = -along_x * along_y * inverse * scale
        for half in range(2):
            damper = jnp.exp(-par[half, 0:1, :] * squared)
            coef[t, half, 0] = straight * damper
            coef[t, half, 1] = mixed * damper
    level_row = lax.broadcasted_iota(jnp.int32, (256, 256), 0)
    level_row = level_row // 128 * 2 + (level_row // 16) % 2
    weight = jnp.zeros((256, 256), F32)
    for level in range(4):
        value = jnp.max(par[level // 2, 4:5, (level % 2) * 16 : (level % 2) * 16 + 16])
        weight = jnp.where(level_row == level, value, weight)
    high, low = split(vert_ref[0] * weight + vert_ref[1] * (1.0 - weight))
    vmat[0] = high
    vmat[1] = low

    sign = jnp.where(lane < 64, 1.0, -1.0)

    def spun(value):
        return pltpu.roll(value, 64, axis=1)

    def doubled(first, second):
        top = jnp.concatenate([first, second], axis=1)
        bottom = jnp.concatenate([spun(first) * sign, spun(second) * sign], axis=1)
        return split(jnp.concatenate([top, bottom], axis=0))

    def column(chunk, local):
        t = chunk * KEYS + local
        even = r1[chunk, pl.ds(local * 2, CHIPS, stride=ROWS), :]
        odd = r1[chunk, pl.ds(local * 2 + 1, CHIPS, stride=ROWS), :]
        halves = [jnp.concatenate([even[h * 64 : h * 64 + 64], odd[h * 64 : h * 64 + 64]], axis=0) for h in range(2)]
        high, low = doubled(*halves)
        step = dot_const_left((slabf_ref[0], slabf_ref[1]), high, low)
        turned = []
        for h in range(2):
            part = step[:, h * 128 : h * 128 + 128]
            turned.append(part * twid_ref[0] + spun(part) * twid_ref[1])
        high, low = split(jnp.concatenate(turned, axis=0))
        modes = dot_const_right(high, low, (mix_ref[0], mix_ref[1]))
        kept = []
        for h in range(2):
            rows = slice(h * 128, h * 128 + 128)
            kept.append(modes[rows, :128] * coef[t, h, 0] + modes[rows, 128:] * coef[t, h, 1])
        high, low = split(jnp.concatenate(kept, axis=1))
        back = dot_const_right(high, low, (vmat[0], vmat[1]))
        turned = []
        for h in range(2):
            part = back[:, h * 128 : h * 128 + 128]
            turned.append(part * twid_ref[0] - spun(part) * twid_ref[1])
        high, low = doubled(*turned)
        result = dot_const_left((slabi_ref[0], slabi_ref[1]), high, low)
        for h in range(2):
            for c in range(2):
                w2[chunk, pl.ds(h * 64 * ROWS + local * 2 + c, 64, stride=ROWS), :] = result[
                    c * 64 : c * 64 + 64, h * 128 : h * 128 + 128
                ]

    for chunk in range(CHUNKS):
        chip_wait(r1, chunk, chip_f_r)
        for local in range(KEYS):
            column(chunk, local)
        chip_send(w2, r2, chunk, chip_b_s, chip_b_r)

    def backward_core(chunk):
        return core_copy(own_b.at[chunk], yb.at[pl.ds(core * 4 + chunk * KEYS, KEYS)], chunk, core_b_s, core_b_r)

    def y_backward(group):
        data = yb[group].T
        high, low = split(data)
        if group < 7:
            c = group + 1
            full = dot_const_right(high, low, (main_ref[0, group], main_ref[1, group]))
            real = full[:64, :128] + full[64:, 128:]
            imag = full[64:, :128] - full[:64, 128:]
            for a in range(9):
                factor = math.cos(2.0 * math.pi * a * c / 16)
                acc_e[a] = factor * real if group == 0 else acc_e[a] + factor * real
            for a in range(1, 8):
                factor = math.sin(2.0 * math.pi * a * c / 16)
                acc_o[a] = factor * imag if group == 0 else acc_o[a] + factor * imag
        else:
            both = dot_const_right(high[:64], low[:64], (packed_ref[0, :, :256], packed_ref[1, :, :256]))
            both = both + dot_const_right(high[64:], low[64:], (packed_ref[0, :, 256:], packed_ref[1, :, 256:]))
            for a in range(9):
                acc_e[a] = acc_e[a] + (both[:, :128] + (-1.0) ** a * both[:, 128:])

    for chunk in range(CHUNKS):
        chip_wait(r2, chunk, chip_b_r)
        for t in range(KEYS):
            own_b[chunk, t] = r2[chunk, pl.ds(t * 2 + other, CHIPS, stride=ROWS), :]
        backward_core(chunk).start()
        for t in range(KEYS):
            yb[core * 4 + chunk * KEYS + t] = r2[chunk, pl.ds(t * 2 + core, CHIPS, stride=ROWS), :]
        backward_core(chunk).wait_recv()
        for group in groups_of(chunk):
            y_backward(group)

    out_ref[:, 0:128] = acc_e[0]
    out_ref[:, 1024:1152] = acc_e[8]
    for a in range(1, 8):
        out_ref[:, a * 128 : a * 128 + 128] = acc_e[a] - acc_o[a]
        out_ref[:, (16 - a) * 128 : (16 - a) * 128 + 128] = acc_e[a] + acc_o[a]

    for chunk in range(CHUNKS):
        forward_core(chunk).wait_send()
        backward_core(chunk).wait_send()
        chip_wait(w1, chunk, chip_f_s)
        chip_wait(w2, chunk, chip_b_s)


def body(cotangent, damping, blending):
    consts = [jnp.asarray(table) for table in tables()]
    anywhere = pl.BlockSpec(memory_space=pltpu.HBM)
    dma = pltpu.SemaphoreType.DMA
    scratch = [
        ((16, 64, 128), F32),
        ((8, 128, 128), F32),
        ((CHUNKS, KEYS, 128, 128), F32),
        ((CHUNKS, CHIPS * ROWS, 128), F32),
        ((CHUNKS, CHIPS * ROWS, 128), F32),
        ((4, 2, 2, 128, 128), F32),
        ((2, 256, 256), BF16),
        ((CHUNKS, CHIPS * ROWS, 128), F32),
        ((CHUNKS, CHIPS * ROWS, 128), F32),
        ((CHUNKS, KEYS, 128, 128), F32),
        ((8, 128, 128), F32),
        ((9, 64, 128), F32),
        ((8, 64, 128), F32),
        ((2, 8, 128), F32),
    ]
    result = pl.pallas_call(
        kernel,
        out_shape=jax.ShapeDtypeStruct((64, NY), F32),
        in_specs=[anywhere] * (3 + len(consts)),
        out_specs=pl.BlockSpec(memory_space=pltpu.VMEM),
        scratch_shapes=[pltpu.VMEM((64, NY), F32), pltpu.SMEM((2,), F32), pltpu.SMEM((2,), F32)]
        + [pltpu.VMEM(c.shape, c.dtype) for c in consts]
        + [pltpu.VMEM(*s) for s in scratch]
        + [dma((CHUNKS,))] * 8
        + [dma, dma, dma, dma((3 + len(consts),))],
        compiler_params=pltpu.CompilerParams(
            collective_id=0, has_side_effects=True, vmem_limit_bytes=62 * 1024 * 1024
        ),
    )(cotangent.reshape(64, NY), damping, blending, *consts)
    return result.reshape(2, 2, 16, NY)


def solution(mesh):
    return jax.shard_map(
        body,
        mesh=mesh,
        in_specs=(P(None, "gz", "gx", None), P("gz"), P("gz")),
        out_specs=P(None, "gz", "gx", None),
        check_vma=False,
    )
```

```python
import functools
import math

import jax
import jax.numpy as jnp
import numpy as np
from jax import lax
from jax.experimental import pallas as pl
from jax.experimental.pallas import tpu as pltpu
from jax.sharding import PartitionSpec as P

NX = 2048
NY = 2048
CHIPS = 128
LANES = 128
GROUPS = 8
CHUNKS = 4
MESH = pl.DeviceIdType.MESH
F32 = jnp.float32
BF16 = jnp.bfloat16


def split_const(table):
    table = np.asarray(table, np.float32)
    high = table.astype(BF16)
    low = (table - high.astype(np.float32)).astype(BF16)
    return np.stack([high, low])


def wave(numerator, period):
    angle = 2.0 * np.pi * (np.asarray(numerator, np.int64) % period) / period
    return np.cos(angle), np.sin(angle)


@functools.cache
def tables():
    d = np.arange(128)[:, None]
    b = np.arange(128)[None, :]
    groups = []
    for c in range(1, 8):
        cos, sin = wave(b * (c + 16 * d), NY)
        groups.append(np.concatenate([cos, -sin], axis=1))
    main = split_const(np.stack(groups))
    half = np.arange(64)[:, None]
    cos0, sin0 = wave(b * (16 * half), NY)
    cos8, sin8 = wave(b * (8 + 16 * half), NY)
    im0 = -sin0
    im0[0] = 1.0 - 2.0 * (np.arange(128) % 2)
    zero = np.zeros((64, 128))
    packed = np.block([[cos0, zero, im0, zero], [zero, cos8, zero, -sin8]])
    packed = split_const(packed)
    core, x_lo, y, z = np.meshgrid(range(2), range(2), range(4), range(8), indexing="ij")
    slab = (x_lo * 64 + z * 8 + y * 2 + core).reshape(-1)
    k1 = np.arange(128)
    cos, sin = wave(k1[:, None] * slab[None, :], 128)
    slab_fwd = split_const(np.concatenate([cos, sin], axis=1))
    slab_inv = split_const(np.concatenate([cos.T, -sin.T], axis=1))
    lane = np.arange(128)
    cos, sin = wave(k1[:, None] * (lane % 16)[None, :], NX)
    sign = np.where(lane < 64, 1.0, -1.0)[None, :]
    twiddle = np.stack([cos, sin * sign]).astype(np.float32)
    src, dst = lane[:, None], lane[None, :]
    same = (src // 16) % 4 == (dst // 16) % 4
    cos, sin = wave((src % 16) * (dst % 16), 16)
    src_im, dst_im = src // 64, dst // 64
    fwd = np.where(src_im == dst_im, cos, np.where(dst_im == 0, sin, -sin)) * same
    inv = np.where(src_im == dst_im, cos, np.where(dst_im == 0, -sin, sin))
    mix = split_const(np.concatenate([fwd, fwd[:, lane ^ 32]], axis=1))
    row = np.arange(256)[:, None]
    col = np.arange(256)[None, :]
    level_row = (row // 128) * 2 + (row // 16) % 2
    level_col = (col // 128) * 2 + (col // 16) % 2
    same_c = (row // 32) % 2 == (col // 32) % 2
    inv = np.tile(inv, (2, 2)) * same_c
    keep = inv * (level_row == level_col)
    carry = inv * (level_row + 1 == level_col)
    vertical = np.stack([keep, carry]).astype(np.float32)
    return main, packed, slab_fwd, slab_inv, twiddle, mix, vertical


def split(value):
    high = value.astype(BF16)
    low = (value - high.astype(F32)).astype(BF16)
    return high, low


def dot(a, b, dims):
    return lax.dot_general(a, b, (dims, ((), ())), preferred_element_type=F32)


def dot_const_left(table, high, low, dims=((1,), (0,))):
    c_high, c_low = table
    return dot(c_high, high, dims) + (dot(c_low, high, dims) + dot(c_high, low, dims))


def dot_const_right(high, low, table, dims=((1,), (0,))):
    c_high, c_low = table
    return dot(high, c_high, dims) + (dot(low, c_high, dims) + dot(high, c_low, dims))


def kernel(
    x_hbm, damp_hbm, blend_hbm, main_hbm, packed_hbm, slabf_hbm, slabi_hbm, twid_hbm, mix_hbm, vert_hbm,
    out_ref,
    x_ref, damp_ref, blend_ref, main_ref, packed_ref, slabf_ref, slabi_ref, twid_ref, mix_ref, vert_ref,
    fold, yf, r1, coef, vmat, w2, yb, acc_e, acc_o, par,
    fwd_s, fwd_r, bwd_s, bwd_r, par_s, par_r, self_f, self_b, load_sem,
):
    gx = lax.axis_index("gx")
    gz = lax.axis_index("gz")
    x_lo, z, y, core = gx // 64, (gx // 8) % 8, (gx // 2) % 4, gx % 2
    x = gz * 2 + x_lo
    me = x * 32 + y * 8 + z
    other = 1 - core

    def for_others(act):
        xs = [(x + dx) % 4 for dx in range(4)]
        ys = [(y + dy) % 4 for dy in range(4)]
        zs = [(z + dz) % 8 for dz in range(8)]
        for dx in (2, 1, 3, 0):
            for dy in (2, 1, 3, 0):
                base = xs[dx] * 32 + ys[dy] * 8
                gbase = (xs[dx] % 2) * 64 + ys[dy] * 2
                for dz in (4, 3, 5, 2, 6, 1, 7, 0):
                    for c in (core, other):
                        if dx or dy or dz or c is other:
                            act(base + zs[dz], c, (gbase + zs[dz] * 8 + c, xs[dx] // 2))

    sources = [x_hbm, main_hbm, packed_hbm, damp_hbm, blend_hbm, slabf_hbm, twid_hbm, mix_hbm, vert_hbm, slabi_hbm]
    targets = [x_ref, main_ref, packed_ref, damp_ref, blend_ref, slabf_ref, twid_ref, mix_ref, vert_ref, slabi_ref]
    loads = [pltpu.make_async_copy(s, t, load_sem.at[i]) for i, (s, t) in enumerate(zip(sources, targets))]
    for load in loads:
        load.start()
    barrier = pltpu.get_barrier_semaphore()

    def signal(chip, c, device):
        pl.semaphore_signal(barrier, inc=1, device_id=device, device_id_type=MESH)

    for_others(signal)

    for load in loads[:3]:
        load.wait()

    def piece(a):
        return x_ref[:, a * 128 : (a + 1) * 128]

    fold[0] = piece(0)
    fold[8] = piece(8)
    for a in range(1, 8):
        first, second = piece(a), piece(16 - a)
        fold[a] = first + second
        fold[8 + a] = first - second

    def y_forward(group):
        if group < 7:
            c = group + 1
            real = fold[0] + (-1.0) ** c * fold[8]
            imag = None
            for a in range(1, 8):
                real = real + math.cos(2.0 * math.pi * a * c / 16) * fold[a]
                term = -math.sin(2.0 * math.pi * a * c / 16) * fold[8 + a]
                imag = term if imag is None else imag + term
            stacked = jnp.concatenate(
                [jnp.concatenate([real, -imag], axis=1), jnp.concatenate([imag, real], axis=1)], axis=0
            )
            table = (main_ref[0, group], main_ref[1, group])
        else:
            even = fold[0] + fold[8]
            for a in (2, 4, 6):
                even = even + fold[a]
            odd = fold[1]
            for a in (3, 5, 7):
                odd = odd + fold[a]
            pair = jnp.concatenate([even + odd, even - odd], axis=1)
            zero = jnp.zeros_like(pair)
            stacked = jnp.concatenate(
                [jnp.concatenate([pair, zero], axis=1), jnp.concatenate([zero, pair], axis=1)], axis=0
            )
            table = (packed_ref[0], packed_ref[1])
        high, low = split(stacked)
        yf[group] = dot_const_left(table, high, low, ((1,), (1,)))

    def forward(chunk):
        target = pl.ds(core * CHIPS + me, 1)

        def go(chip, c, device):
            pltpu.make_async_remote_copy(
                src_ref=yf.at[c * 4 + chunk, pl.ds(chip, 1)], dst_ref=r1.at[chunk, target],
                send_sem=fwd_s.at[chunk], recv_sem=fwd_r.at[chunk], device_id=device, device_id_type=MESH,
            ).start()

        forward_self(chunk).start()
        for_others(go)

    def forward_self(chunk):
        own = yf.at[core * 4 + chunk, pl.ds(me, 1)]
        return pltpu.make_async_copy(own, r1.at[chunk, pl.ds(core * CHIPS + me, 1)], self_f.at[chunk])

    def backward(chunk):
        target = pl.ds(me, 1)

        def go(chip, c, device):
            pltpu.make_async_remote_copy(
                src_ref=w2.at[chunk, pl.ds(c * CHIPS + chip, 1)], dst_ref=yb.at[core * 4 + chunk, target],
                send_sem=bwd_s.at[chunk], recv_sem=bwd_r.at[chunk], device_id=device, device_id_type=MESH,
            ).start()

        backward_self(chunk).start()
        for_others(go)

    def backward_self(chunk):
        own = w2.at[chunk, pl.ds(core * CHIPS + me, 1)]
        return pltpu.make_async_copy(own, yb.at[core * 4 + chunk, pl.ds(me, 1)], self_b.at[chunk])

    def wait_others(sem, chunk):
        most = r1.at[0, pl.ds(0, 255)]
        pltpu.make_async_copy(most, most, sem.at[chunk]).wait()

    y_forward(0)
    y_forward(4)
    pl.semaphore_wait(barrier, 255)
    forward(0)
    for load in loads[3:]:
        load.wait()
    lane = lax.broadcasted_iota(jnp.int32, (8, 128), 1)
    row8 = lax.broadcasted_iota(jnp.int32, (8, 128), 0)
    upper = (lane // 16) % 2 == 1
    par[gz] = jnp.where(
        row8 < 4,
        jnp.where(upper, damp_ref[1], damp_ref[0]),
        jnp.where(upper, blend_ref[1], blend_ref[0]),
    )
    par_copy = pltpu.make_async_remote_copy(
        src_ref=par.at[gz], dst_ref=par.at[gz], send_sem=par_s, recv_sem=par_r,
        device_id=(gx, 1 - gz), device_id_type=MESH,
    )
    par_copy.start()

    for chunk in range(1, CHUNKS):
        y_forward(chunk)
        y_forward(chunk + 4)
        forward(chunk)

    par_copy.wait()
    lane = lax.broadcasted_iota(jnp.int32, (128, 128), 1)
    mode = lax.broadcasted_iota(jnp.int32, (128, 128), 0) + 128 * (lane % 16)
    wave_x = jnp.where(mode < NX // 2, mode, mode - NX)
    wave_x = jnp.where(mode == NX // 2, 0, wave_x)
    along_x = (2.0 * math.pi / NX) * wave_x.astype(F32)
    second = (lane // 32) % 2 == 1
    for t in range(4):
        group = core * 4 + t
        slot = jnp.where(me < 64, me * 16, 8 + (me - 64) * 16)
        number = jnp.where(group == 7, slot, group + 1 + 16 * me)
        number = jnp.where(number < NY // 2, number, number - NY)
        once = jnp.logical_and(group == 7, me == 0)
        scale = jnp.where(once, 1.0, 2.0) * (1.0 / (NX * NY))
        along_y = jnp.full((128, 128), (2.0 * math.pi / NY) * number.astype(F32))
        squared = along_x * along_x + along_y * along_y
        anchor = squared == 0.0
        inverse = jnp.where(anchor, 0.0, 1.0 / jnp.where(anchor, 1.0, squared))
        cross = jnp.where(second, along_x, along_y)
        straight = jnp.where(anchor, 1.0, cross * cross * inverse) * scale
        mixed = -along_x * along_y * inverse * scale
        for half in range(2):
            damper = jnp.exp(-par[half, 0:1, :] * squared)
            coef[t, half, 0] = straight * damper
            coef[t, half, 1] = mixed * damper
    level_row = lax.broadcasted_iota(jnp.int32, (256, 256), 0)
    level_row = level_row // 128 * 2 + (level_row // 16) % 2
    weight = jnp.zeros((256, 256), F32)
    for level in range(4):
        value = jnp.max(par[level // 2, 4:5, (level % 2) * 16 : (level % 2) * 16 + 16])
        weight = jnp.where(level_row == level, value, weight)
    high, low = split(vert_ref[0] * weight + vert_ref[1] * (1.0 - weight))
    vmat[0] = high
    vmat[1] = low

    sign = jnp.where(lane < 64, 1.0, -1.0)

    def spun(value):
        return pltpu.roll(value, 64, axis=1)

    def doubled(first, second):
        top = jnp.concatenate([first, second], axis=1)
        bottom = jnp.concatenate([spun(first) * sign, spun(second) * sign], axis=1)
        return split(jnp.concatenate([top, bottom], axis=0))

    def column(t):
        halves = [
            jnp.concatenate([r1[t, h * 64 : h * 64 + 64], r1[t, CHIPS + h * 64 : CHIPS + h * 64 + 64]], axis=0)
            for h in range(2)
        ]
        high, low = doubled(*halves)
        step = dot_const_left((slabf_ref[0], slabf_ref[1]), high, low)
        turned = []
        for h in range(2):
            part = step[:, h * 128 : h * 128 + 128]
            turned.append(part * twid_ref[0] + spun(part) * twid_ref[1])
        high, low = split(jnp.concatenate(turned, axis=0))
        modes = dot_const_right(high, low, (mix_ref[0], mix_ref[1]))
        kept = []
        for h in range(2):
            rows = slice(h * 128, h * 128 + 128)
            kept.append(modes[rows, :128] * coef[t, h, 0] + modes[rows, 128:] * coef[t, h, 1])
        high, low = split(jnp.concatenate(kept, axis=1))
        back = dot_const_right(high, low, (vmat[0], vmat[1]))
        turned = []
        for h in range(2):
            part = back[:, h * 128 : h * 128 + 128]
            turned.append(part * twid_ref[0] - spun(part) * twid_ref[1])
        high, low = doubled(*turned)
        result = dot_const_left((slabi_ref[0], slabi_ref[1]), high, low)
        for h in range(2):
            for c in range(2):
                w2[t, c * CHIPS + h * 64 : c * CHIPS + h * 64 + 64] = result[c * 64 : c * 64 + 64, h * 128 : h * 128 + 128]

    for chunk in range(CHUNKS):
        wait_others(fwd_r, chunk)
        forward_self(chunk).wait()
        column(chunk)
        backward(chunk)

    def y_backward(group):
        data = yb[group].T
        high, low = split(data)
        if group < 7:
            c = group + 1
            full = dot_const_right(high, low, (main_ref[0, group], main_ref[1, group]))
            real = full[:64, :128] + full[64:, 128:]
            imag = full[64:, :128] - full[:64, 128:]
            for a in range(9):
                factor = math.cos(2.0 * math.pi * a * c / 16)
                acc_e[a] = factor * real if group == 0 else acc_e[a] + factor * real
            for a in range(1, 8):
                factor = math.sin(2.0 * math.pi * a * c / 16)
                acc_o[a] = factor * imag if group == 0 else acc_o[a] + factor * imag
        else:
            both = dot_const_right(high[:64], low[:64], (packed_ref[0, :, :256], packed_ref[1, :, :256]))
            both = both + dot_const_right(high[64:], low[64:], (packed_ref[0, :, 256:], packed_ref[1, :, 256:]))
            for a in range(9):
                acc_e[a] = acc_e[a] + (both[:, :128] + (-1.0) ** a * both[:, 128:])

    for chunk in range(CHUNKS):
        wait_others(bwd_r, chunk)
        backward_self(chunk).wait()
        y_backward(chunk)
        y_backward(chunk + 4)

    out_ref[:, 0:128] = acc_e[0]
    out_ref[:, 1024:1152] = acc_e[8]
    for a in range(1, 8):
        out_ref[:, a * 128 : a * 128 + 128] = acc_e[a] - acc_o[a]
        out_ref[:, (16 - a) * 128 : (16 - a) * 128 + 128] = acc_e[a] + acc_o[a]

    for chunk in range(CHUNKS):
        wait_others(fwd_s, chunk)
        wait_others(bwd_s, chunk)


def body(cotangent, damping, blending):
    consts = [jnp.asarray(table) for table in tables()]
    anywhere = pl.BlockSpec(memory_space=pltpu.HBM)
    dma = pltpu.SemaphoreType.DMA
    scratch = [
        ((16, 64, 128), F32),
        ((8, 128, 128), F32),
        ((CHUNKS, 2 * CHIPS, 128), F32),
        ((4, 2, 2, 128, 128), F32),
        ((2, 256, 256), BF16),
        ((CHUNKS, 2 * CHIPS, 128), F32),
        ((8, 128, 128), F32),
        ((9, 64, 128), F32),
        ((8, 64, 128), F32),
        ((2, 8, 128), F32),
    ]
    result = pl.pallas_call(
        kernel,
        out_shape=jax.ShapeDtypeStruct((64, NY), F32),
        in_specs=[anywhere] * (3 + len(consts)),
        out_specs=pl.BlockSpec(memory_space=pltpu.VMEM),
        scratch_shapes=[pltpu.VMEM((64, NY), F32), pltpu.SMEM((2,), F32), pltpu.SMEM((2,), F32)]
        + [pltpu.VMEM(c.shape, c.dtype) for c in consts]
        + [pltpu.VMEM(*s) for s in scratch]
        + [dma((CHUNKS,))] * 4
        + [dma, dma, dma((CHUNKS,)), dma((CHUNKS,)), dma((3 + len(consts),))],
        compiler_params=pltpu.CompilerParams(
            collective_id=0, has_side_effects=True, vmem_limit_bytes=62 * 1024 * 1024
        ),
    )(cotangent.reshape(64, NY), damping, blending, *consts)
    return result.reshape(2, 2, 16, NY)


def solution(mesh):
    return jax.shard_map(
        body,
        mesh=mesh,
        in_specs=(P(None, "gz", "gx", None), P("gz"), P("gz")),
        out_specs=P(None, "gz", "gx", None),
        check_vma=False,
    )
```

```python
import functools
import math

import jax
import jax.numpy as jnp
import numpy as np
from jax import lax
from jax.experimental import pallas as pl
from jax.experimental.pallas import tpu as pltpu
from jax.sharding import PartitionSpec as P

NX = 2048
NY = 2048
CHIPS = 128
LANES = 128
GROUPS = 8
CHUNKS = 4
MESH = pl.DeviceIdType.MESH
F32 = jnp.float32
BF16 = jnp.bfloat16


def split_const(table):
    table = np.asarray(table, np.float32)
    high = table.astype(BF16)
    low = (table - high.astype(np.float32)).astype(BF16)
    return np.stack([high, low])


def wave(numerator, period):
    angle = 2.0 * np.pi * (np.asarray(numerator, np.int64) % period) / period
    return np.cos(angle), np.sin(angle)


@functools.cache
def tables():
    d = np.arange(128)[:, None]
    b = np.arange(128)[None, :]
    groups = []
    for c in range(1, 8):
        cos, sin = wave(b * (c + 16 * d), NY)
        groups.append(np.concatenate([cos, -sin], axis=1))
    main = split_const(np.stack(groups))
    half = np.arange(64)[:, None]
    cos0, sin0 = wave(b * (16 * half), NY)
    cos8, sin8 = wave(b * (8 + 16 * half), NY)
    im0 = -sin0
    im0[0] = 1.0 - 2.0 * (np.arange(128) % 2)
    zero = np.zeros((64, 128))
    packed = np.block([[cos0, zero, im0, zero], [zero, cos8, zero, -sin8]])
    packed = split_const(packed)
    core, x_lo, y, z = np.meshgrid(range(2), range(2), range(4), range(8), indexing="ij")
    slab = (x_lo * 64 + z * 8 + y * 2 + core).reshape(-1)
    k1 = np.arange(128)
    cos, sin = wave(k1[:, None] * slab[None, :], 128)
    slab_fwd = split_const(np.concatenate([cos, sin], axis=1))
    slab_inv = split_const(np.concatenate([cos.T, -sin.T], axis=1))
    lane = np.arange(128)
    cos, sin = wave(k1[:, None] * (lane % 16)[None, :], NX)
    sign = np.where(lane < 64, 1.0, -1.0)[None, :]
    twiddle = np.stack([cos, sin * sign]).astype(np.float32)
    src, dst = lane[:, None], lane[None, :]
    same = (src // 16) % 4 == (dst // 16) % 4
    cos, sin = wave((src % 16) * (dst % 16), 16)
    src_im, dst_im = src // 64, dst // 64
    fwd = np.where(src_im == dst_im, cos, np.where(dst_im == 0, sin, -sin)) * same
    inv = np.where(src_im == dst_im, cos, np.where(dst_im == 0, -sin, sin))
    mix = split_const(np.concatenate([fwd, fwd[:, lane ^ 32]], axis=1))
    row = np.arange(256)[:, None]
    col = np.arange(256)[None, :]
    level_row = (row // 128) * 2 + (row // 16) % 2
    level_col = (col // 128) * 2 + (col // 16) % 2
    same_c = (row // 32) % 2 == (col // 32) % 2
    inv = np.tile(inv, (2, 2)) * same_c
    keep = inv * (level_row == level_col)
    carry = inv * (level_row + 1 == level_col)
    vertical = np.stack([keep, carry]).astype(np.float32)
    return main, packed, slab_fwd, slab_inv, twiddle, mix, vertical


def split(value):
    high = value.astype(BF16)
    low = (value - high.astype(F32)).astype(BF16)
    return high, low


def dot(a, b, dims):
    return lax.dot_general(a, b, (dims, ((), ())), preferred_element_type=F32)


def dot_const_left(table, high, low, dims=((1,), (0,))):
    c_high, c_low = table
    return dot(c_high, high, dims) + (dot(c_low, high, dims) + dot(c_high, low, dims))


def dot_const_right(high, low, table, dims=((1,), (0,))):
    c_high, c_low = table
    return dot(high, c_high, dims) + (dot(low, c_high, dims) + dot(high, c_low, dims))


def kernel(
    x_hbm, damp_hbm, blend_hbm, main_hbm, packed_hbm, slabf_hbm, slabi_hbm, twid_hbm, mix_hbm, vert_hbm,
    out_ref,
    x_ref, damp_ref, blend_ref, main_ref, packed_ref, slabf_ref, slabi_ref, twid_ref, mix_ref, vert_ref,
    fold, yf, r1, coef, vmat, w2, yb, acc_e, acc_o, par,
    fwd_s, fwd_r, bwd_s, bwd_r, par_s, par_r, self_f, self_b, load_sem, pair_sem,
):
    gx = lax.axis_index("gx")
    gz = lax.axis_index("gz")
    x_lo, z, y, core = gx // 64, (gx // 8) % 8, (gx // 2) % 4, gx % 2
    x = gz * 2 + x_lo
    me = x * 32 + y * 8 + z
    other = 1 - core

    def for_others(act, cores=None):
        cores = (core, other) if cores is None else cores
        xs = [(x + dx) % 4 for dx in range(4)]
        ys = [(y + dy) % 4 for dy in range(4)]
        zs = [(z + dz) % 8 for dz in range(8)]
        for dx in (2, 1, 3, 0):
            for dy in (2, 1, 3, 0):
                base = xs[dx] * 32 + ys[dy] * 8
                gbase = (xs[dx] % 2) * 64 + ys[dy] * 2
                for dz in (4, 3, 5, 2, 6, 1, 7, 0):
                    for c in cores:
                        if dx or dy or dz or c is other:
                            act(base + zs[dz], c, (gbase + zs[dz] * 8 + c, xs[dx] // 2))

    sources = [x_hbm, main_hbm, packed_hbm, damp_hbm, blend_hbm, slabf_hbm, twid_hbm, mix_hbm, vert_hbm, slabi_hbm]
    targets = [x_ref, main_ref, packed_ref, damp_ref, blend_ref, slabf_ref, twid_ref, mix_ref, vert_ref, slabi_ref]
    loads = [pltpu.make_async_copy(s, t, load_sem.at[i]) for i, (s, t) in enumerate(zip(sources, targets))]
    for load in loads:
        load.start()
    barrier = pltpu.get_barrier_semaphore()

    def signal(chip, c, device):
        pl.semaphore_signal(barrier, inc=1, device_id=device, device_id_type=MESH)

    for_others(signal, (core,))
    sibling = (gx + 1 - 2 * core, gz)
    signal(me, other, sibling)

    for load in loads[:3]:
        load.wait()

    def piece(a):
        return x_ref[:, a * 128 : (a + 1) * 128]

    fold[0] = piece(0)
    fold[8] = piece(8)
    for a in range(1, 8):
        first, second = piece(a), piece(16 - a)
        fold[a] = first + second
        fold[8 + a] = first - second

    def y_forward(group):
        if group < 7:
            c = group + 1
            real = fold[0] + (-1.0) ** c * fold[8]
            imag = None
            for a in range(1, 8):
                real = real + math.cos(2.0 * math.pi * a * c / 16) * fold[a]
                term = -math.sin(2.0 * math.pi * a * c / 16) * fold[8 + a]
                imag = term if imag is None else imag + term
            stacked = jnp.concatenate(
                [jnp.concatenate([real, -imag], axis=1), jnp.concatenate([imag, real], axis=1)], axis=0
            )
            table = (main_ref[0, group], main_ref[1, group])
        else:
            even = fold[0] + fold[8]
            for a in (2, 4, 6):
                even = even + fold[a]
            odd = fold[1]
            for a in (3, 5, 7):
                odd = odd + fold[a]
            pair = jnp.concatenate([even + odd, even - odd], axis=1)
            zero = jnp.zeros_like(pair)
            stacked = jnp.concatenate(
                [jnp.concatenate([pair, zero], axis=1), jnp.concatenate([zero, pair], axis=1)], axis=0
            )
            table = (packed_ref[0], packed_ref[1])
        high, low = split(stacked)
        yf[group] = dot_const_left(table, high, low, ((1,), (1,)))

    def forward(chunk, apart=False):
        target = pl.ds(core * CHIPS + me, 1)

        def go(chip, c, device):
            pltpu.make_async_remote_copy(
                src_ref=yf.at[c * 4 + chunk, pl.ds(chip, 1)], dst_ref=r1.at[chunk, target],
                send_sem=fwd_s.at[chunk], recv_sem=fwd_r.at[chunk], device_id=device, device_id_type=MESH,
            ).start()

        forward_self(chunk).start()
        if apart:
            for_others(go, (core,))
            pl.semaphore_wait(pair_sem, 1)
            for_others(go, (other,))
        else:
            for_others(go)

    def forward_self(chunk):
        own = yf.at[core * 4 + chunk, pl.ds(me, 1)]
        return pltpu.make_async_copy(own, r1.at[chunk, pl.ds(core * CHIPS + me, 1)], self_f.at[chunk])

    def backward(chunk):
        target = pl.ds(me, 1)

        def go(chip, c, device):
            pltpu.make_async_remote_copy(
                src_ref=w2.at[chunk, pl.ds(c * CHIPS + chip, 1)], dst_ref=yb.at[core * 4 + chunk, target],
                send_sem=bwd_s.at[chunk], recv_sem=bwd_r.at[chunk], device_id=device, device_id_type=MESH,
            ).start()

        backward_self(chunk).start()
        for_others(go)

    def backward_self(chunk):
        own = w2.at[chunk, pl.ds(core * CHIPS + me, 1)]
        return pltpu.make_async_copy(own, yb.at[core * 4 + chunk, pl.ds(me, 1)], self_b.at[chunk])

    def wait_others(sem, chunk):
        most = r1.at[0, pl.ds(0, 255)]
        pltpu.make_async_copy(most, most, sem.at[chunk]).wait()

    y_forward(0)
    y_forward(4)
    pl.semaphore_wait(barrier, 128)
    pl.semaphore_signal(pair_sem, inc=1, device_id=sibling, device_id_type=MESH)
    forward(0, True)
    for load in loads[3:]:
        load.wait()
    lane = lax.broadcasted_iota(jnp.int32, (8, 128), 1)
    row8 = lax.broadcasted_iota(jnp.int32, (8, 128), 0)
    upper = (lane // 16) % 2 == 1
    par[gz] = jnp.where(
        row8 < 4,
        jnp.where(upper, damp_ref[1], damp_ref[0]),
        jnp.where(upper, blend_ref[1], blend_ref[0]),
    )
    par_copy = pltpu.make_async_remote_copy(
        src_ref=par.at[gz], dst_ref=par.at[gz], send_sem=par_s, recv_sem=par_r,
        device_id=(gx, 1 - gz), device_id_type=MESH,
    )
    par_copy.start()

    for chunk in range(1, CHUNKS):
        y_forward(chunk)
        y_forward(chunk + 4)
        forward(chunk)

    par_copy.wait()
    lane = lax.broadcasted_iota(jnp.int32, (128, 128), 1)
    mode = lax.broadcasted_iota(jnp.int32, (128, 128), 0) + 128 * (lane % 16)
    wave_x = jnp.where(mode < NX // 2, mode, mode - NX)
    wave_x = jnp.where(mode == NX // 2, 0, wave_x)
    along_x = (2.0 * math.pi / NX) * wave_x.astype(F32)
    second = (lane // 32) % 2 == 1
    for t in range(4):
        group = core * 4 + t
        slot = jnp.where(me < 64, me * 16, 8 + (me - 64) * 16)
        number = jnp.where(group == 7, slot, group + 1 + 16 * me)
        number = jnp.where(number < NY // 2, number, number - NY)
        once = jnp.logical_and(group == 7, me == 0)
        scale = jnp.where(once, 1.0, 2.0) * (1.0 / (NX * NY))
        along_y = jnp.full((128, 128), (2.0 * math.pi / NY) * number.astype(F32))
        squared = along_x * along_x + along_y * along_y
        anchor = squared == 0.0
        inverse = jnp.where(anchor, 0.0, 1.0 / jnp.where(anchor, 1.0, squared))
        cross = jnp.where(second, along_x, along_y)
        straight = jnp.where(anchor, 1.0, cross * cross * inverse) * scale
        mixed = -along_x * along_y * inverse * scale
        for half in range(2):
            damper = jnp.exp(-par[half, 0:1, :] * squared)
            coef[t, half, 0] = straight * damper
            coef[t, half, 1] = mixed * damper
    level_row = lax.broadcasted_iota(jnp.int32, (256, 256), 0)
    level_row = level_row // 128 * 2 + (level_row // 16) % 2
    weight = jnp.zeros((256, 256), F32)
    for level in range(4):
        value = jnp.max(par[level // 2, 4:5, (level % 2) * 16 : (level % 2) * 16 + 16])
        weight = jnp.where(level_row == level, value, weight)
    high, low = split(vert_ref[0] * weight + vert_ref[1] * (1.0 - weight))
    vmat[0] = high
    vmat[1] = low

    sign = jnp.where(lane < 64, 1.0, -1.0)

    def spun(value):
        return pltpu.roll(value, 64, axis=1)

    def doubled(first, second):
        top = jnp.concatenate([first, second], axis=1)
        bottom = jnp.concatenate([spun(first) * sign, spun(second) * sign], axis=1)
        return split(jnp.concatenate([top, bottom], axis=0))

    def column(t):
        halves = [
            jnp.concatenate([r1[t, h * 64 : h * 64 + 64], r1[t, CHIPS + h * 64 : CHIPS + h * 64 + 64]], axis=0)
            for h in range(2)
        ]
        high, low = doubled(*halves)
        step = dot_const_left((slabf_ref[0], slabf_ref[1]), high, low)
        turned = []
        for h in range(2):
            part = step[:, h * 128 : h * 128 + 128]
            turned.append(part * twid_ref[0] + spun(part) * twid_ref[1])
        high, low = split(jnp.concatenate(turned, axis=0))
        modes = dot_const_right(high, low, (mix_ref[0], mix_ref[1]))
        kept = []
        for h in range(2):
            rows = slice(h * 128, h * 128 + 128)
            kept.append(modes[rows, :128] * coef[t, h, 0] + modes[rows, 128:] * coef[t, h, 1])
        high, low = split(jnp.concatenate(kept, axis=1))
        back = dot_const_right(high, low, (vmat[0], vmat[1]))
        turned = []
        for h in range(2):
            part = back[:, h * 128 : h * 128 + 128]
            turned.append(part * twid_ref[0] - spun(part) * twid_ref[1])
        high, low = doubled(*turned)
        result = dot_const_left((slabi_ref[0], slabi_ref[1]), high, low)
        for h in range(2):
            for c in range(2):
                w2[t, c * CHIPS + h * 64 : c * CHIPS + h * 64 + 64] = result[c * 64 : c * 64 + 64, h * 128 : h * 128 + 128]

    for chunk in range(CHUNKS):
        wait_others(fwd_r, chunk)
        forward_self(chunk).wait()
        column(chunk)
        backward(chunk)

    def y_backward(group):
        data = yb[group].T
        high, low = split(data)
        if group < 7:
            c = group + 1
            full = dot_const_right(high, low, (main_ref[0, group], main_ref[1, group]))
            real = full[:64, :128] + full[64:, 128:]
            imag = full[64:, :128] - full[:64, 128:]
            for a in range(9):
                factor = math.cos(2.0 * math.pi * a * c / 16)
                acc_e[a] = factor * real if group == 0 else acc_e[a] + factor * real
            for a in range(1, 8):
                factor = math.sin(2.0 * math.pi * a * c / 16)
                acc_o[a] = factor * imag if group == 0 else acc_o[a] + factor * imag
        else:
            both = dot_const_right(high[:64], low[:64], (packed_ref[0, :, :256], packed_ref[1, :, :256]))
            both = both + dot_const_right(high[64:], low[64:], (packed_ref[0, :, 256:], packed_ref[1, :, 256:]))
            for a in range(9):
                acc_e[a] = acc_e[a] + (both[:, :128] + (-1.0) ** a * both[:, 128:])

    for chunk in range(CHUNKS):
        wait_others(bwd_r, chunk)
        backward_self(chunk).wait()
        y_backward(chunk)
        y_backward(chunk + 4)

    out_ref[:, 0:128] = acc_e[0]
    out_ref[:, 1024:1152] = acc_e[8]
    for a in range(1, 8):
        out_ref[:, a * 128 : a * 128 + 128] = acc_e[a] - acc_o[a]
        out_ref[:, (16 - a) * 128 : (16 - a) * 128 + 128] = acc_e[a] + acc_o[a]

    for chunk in range(CHUNKS):
        wait_others(fwd_s, chunk)
        wait_others(bwd_s, chunk)


def body(cotangent, damping, blending):
    consts = [jnp.asarray(table) for table in tables()]
    anywhere = pl.BlockSpec(memory_space=pltpu.HBM)
    dma = pltpu.SemaphoreType.DMA
    scratch = [
        ((16, 64, 128), F32),
        ((8, 128, 128), F32),
        ((CHUNKS, 2 * CHIPS, 128), F32),
        ((4, 2, 2, 128, 128), F32),
        ((2, 256, 256), BF16),
        ((CHUNKS, 2 * CHIPS, 128), F32),
        ((8, 128, 128), F32),
        ((9, 64, 128), F32),
        ((8, 64, 128), F32),
        ((2, 8, 128), F32),
    ]
    result = pl.pallas_call(
        kernel,
        out_shape=jax.ShapeDtypeStruct((64, NY), F32),
        in_specs=[anywhere] * (3 + len(consts)),
        out_specs=pl.BlockSpec(memory_space=pltpu.VMEM),
        scratch_shapes=[pltpu.VMEM((64, NY), F32), pltpu.SMEM((2,), F32), pltpu.SMEM((2,), F32)]
        + [pltpu.VMEM(c.shape, c.dtype) for c in consts]
        + [pltpu.VMEM(*s) for s in scratch]
        + [dma((CHUNKS,))] * 4
        + [dma, dma, dma((CHUNKS,)), dma((CHUNKS,)), dma((3 + len(consts),)), pltpu.SemaphoreType.REGULAR],
        compiler_params=pltpu.CompilerParams(
            collective_id=0, has_side_effects=True, vmem_limit_bytes=62 * 1024 * 1024
        ),
    )(cotangent.reshape(64, NY), damping, blending, *consts)
    return result.reshape(2, 2, 16, NY)


def solution(mesh):
    return jax.shard_map(
        body,
        mesh=mesh,
        in_specs=(P(None, "gz", "gx", None), P("gz"), P("gz")),
        out_specs=P(None, "gz", "gx", None),
        check_vma=False,
    )
```

```python
import functools
import math

import jax
import jax.numpy as jnp
import numpy as np
from jax import lax
from jax.experimental import pallas as pl
from jax.experimental.pallas import tpu as pltpu
from jax.sharding import PartitionSpec as P

NX = 2048
NY = 2048
CHIPS = 128
LANES = 128
GROUPS = 8
CHUNKS = 4
MESH = pl.DeviceIdType.MESH
F32 = jnp.float32
BF16 = jnp.bfloat16


def split_const(table):
    table = np.asarray(table, np.float32)
    high = table.astype(BF16)
    low = (table - high.astype(np.float32)).astype(BF16)
    return np.stack([high, low])


def wave(numerator, period):
    angle = 2.0 * np.pi * (np.asarray(numerator, np.int64) % period) / period
    return np.cos(angle), np.sin(angle)


@functools.cache
def tables():
    d = np.arange(128)[:, None]
    b = np.arange(128)[None, :]
    groups = []
    for c in range(1, 8):
        cos, sin = wave(b * (c + 16 * d), NY)
        groups.append(np.concatenate([cos, -sin], axis=1))
    main = split_const(np.stack(groups))
    half = np.arange(64)[:, None]
    cos0, sin0 = wave(b * (16 * half), NY)
    cos8, sin8 = wave(b * (8 + 16 * half), NY)
    im0 = -sin0
    im0[0] = 1.0 - 2.0 * (np.arange(128) % 2)
    zero = np.zeros((64, 128))
    packed = np.block([[cos0, zero, im0, zero], [zero, cos8, zero, -sin8]])
    packed = split_const(packed)
    core, x_lo, y, z = np.meshgrid(range(2), range(2), range(4), range(8), indexing="ij")
    slab = (x_lo * 64 + z * 8 + y * 2 + core).reshape(-1)
    k1 = np.arange(128)
    cos, sin = wave(k1[:, None] * slab[None, :], 128)
    slab_fwd = split_const(np.concatenate([cos, sin], axis=1))
    slab_inv = split_const(np.concatenate([cos.T, -sin.T], axis=1))
    lane = np.arange(128)
    cos, sin = wave(k1[:, None] * (lane % 16)[None, :], NX)
    sign = np.where(lane < 64, 1.0, -1.0)[None, :]
    twiddle = np.stack([cos, sin * sign]).astype(np.float32)
    src, dst = lane[:, None], lane[None, :]
    same = (src // 16) % 4 == (dst // 16) % 4
    cos, sin = wave((src % 16) * (dst % 16), 16)
    src_im, dst_im = src // 64, dst // 64
    fwd = np.where(src_im == dst_im, cos, np.where(dst_im == 0, sin, -sin)) * same
    inv = np.where(src_im == dst_im, cos, np.where(dst_im == 0, -sin, sin))
    mix = split_const(np.concatenate([fwd, fwd[:, lane ^ 32]], axis=1))
    row = np.arange(256)[:, None]
    col = np.arange(256)[None, :]
    level_row = (row // 128) * 2 + (row // 16) % 2
    level_col = (col // 128) * 2 + (col // 16) % 2
    same_c = (row // 32) % 2 == (col // 32) % 2
    inv = np.tile(inv, (2, 2)) * same_c
    keep = inv * (level_row == level_col)
    carry = inv * (level_row + 1 == level_col)
    vertical = np.stack([keep, carry]).astype(np.float32)
    return main, packed, slab_fwd, slab_inv, twiddle, mix, vertical


def split(value):
    high = value.astype(BF16)
    low = (value - high.astype(F32)).astype(BF16)
    return high, low


def dot(a, b, dims):
    return lax.dot_general(a, b, (dims, ((), ())), preferred_element_type=F32)


def dot_const_left(table, high, low, dims=((1,), (0,))):
    c_high, c_low = table
    return dot(c_high, high, dims) + (dot(c_low, high, dims) + dot(c_high, low, dims))


def dot_const_right(high, low, table, dims=((1,), (0,))):
    c_high, c_low = table
    return dot(high, c_high, dims) + (dot(low, c_high, dims) + dot(high, c_low, dims))


def kernel(
    x_hbm, damp_hbm, blend_hbm, main_hbm, packed_hbm, slabf_hbm, slabi_hbm, twid_hbm, mix_hbm, vert_hbm,
    out_ref,
    x_ref, damp_ref, blend_ref, main_ref, packed_ref, slabf_ref, slabi_ref, twid_ref, mix_ref, vert_ref,
    fold, yf, r1, coef, vmat, w2, yb, acc_e, acc_o, par,
    fwd_s, fwd_r, bwd_s, bwd_r, par_s, par_r, self_f, self_b, load_sem, pair_sem,
):
    gx = lax.axis_index("gx")
    gz = lax.axis_index("gz")
    x_lo, z, y, core = gx // 64, (gx // 8) % 8, (gx // 2) % 4, gx % 2
    x = gz * 2 + x_lo
    me = x * 32 + y * 8 + z
    other = 1 - core

    def for_others(act, cores=None):
        cores = (core, other) if cores is None else cores
        xs = [(x + dx) % 4 for dx in range(4)]
        ys = [(y + dy) % 4 for dy in range(4)]
        zs = [(z + dz) % 8 for dz in range(8)]
        for c in cores:
            for dx in (2, 1, 3, 0):
                for dy in (2, 1, 3, 0):
                    base = xs[dx] * 32 + ys[dy] * 8
                    gbase = (xs[dx] % 2) * 64 + ys[dy] * 2
                    for dz in (4, 3, 5, 2, 6, 1, 7, 0):
                        if dx or dy or dz or c is other:
                            act(base + zs[dz], c, (gbase + zs[dz] * 8 + c, xs[dx] // 2))

    sources = [x_hbm, main_hbm, packed_hbm, damp_hbm, blend_hbm, slabf_hbm, twid_hbm, mix_hbm, vert_hbm, slabi_hbm]
    targets = [x_ref, main_ref, packed_ref, damp_ref, blend_ref, slabf_ref, twid_ref, mix_ref, vert_ref, slabi_ref]
    loads = [pltpu.make_async_copy(s, t, load_sem.at[i]) for i, (s, t) in enumerate(zip(sources, targets))]
    for load in loads:
        load.start()
    barrier = pltpu.get_barrier_semaphore()

    def signal(chip, c, device):
        pl.semaphore_signal(barrier, inc=1, device_id=device, device_id_type=MESH)

    for_others(signal, (core,))
    sibling = (gx + 1 - 2 * core, gz)
    signal(me, other, sibling)

    for load in loads[:3]:
        load.wait()

    def piece(a):
        return x_ref[:, a * 128 : (a + 1) * 128]

    fold[0] = piece(0)
    fold[8] = piece(8)
    for a in range(1, 8):
        first, second = piece(a), piece(16 - a)
        fold[a] = first + second
        fold[8 + a] = first - second

    def y_forward(group):
        if group < 7:
            c = group + 1
            real = fold[0] + (-1.0) ** c * fold[8]
            imag = None
            for a in range(1, 8):
                real = real + math.cos(2.0 * math.pi * a * c / 16) * fold[a]
                term = -math.sin(2.0 * math.pi * a * c / 16) * fold[8 + a]
                imag = term if imag is None else imag + term
            stacked = jnp.concatenate(
                [jnp.concatenate([real, -imag], axis=1), jnp.concatenate([imag, real], axis=1)], axis=0
            )
            table = (main_ref[0, group], main_ref[1, group])
        else:
            even = fold[0] + fold[8]
            for a in (2, 4, 6):
                even = even + fold[a]
            odd = fold[1]
            for a in (3, 5, 7):
                odd = odd + fold[a]
            pair = jnp.concatenate([even + odd, even - odd], axis=1)
            zero = jnp.zeros_like(pair)
            stacked = jnp.concatenate(
                [jnp.concatenate([pair, zero], axis=1), jnp.concatenate([zero, pair], axis=1)], axis=0
            )
            table = (packed_ref[0], packed_ref[1])
        high, low = split(stacked)
        yf[group] = dot_const_left(table, high, low, ((1,), (1,)))

    def forward(chunk, apart=False):
        target = pl.ds(core * CHIPS + me, 1)

        def go(chip, c, device):
            pltpu.make_async_remote_copy(
                src_ref=yf.at[c * 4 + chunk, pl.ds(chip, 1)], dst_ref=r1.at[chunk, target],
                send_sem=fwd_s.at[chunk], recv_sem=fwd_r.at[chunk], device_id=device, device_id_type=MESH,
            ).start()

        forward_self(chunk).start()
        if apart:
            for_others(go, (core,))
            pl.semaphore_wait(pair_sem, 1)
            for_others(go, (other,))
        else:
            for_others(go)

    def forward_self(chunk):
        own = yf.at[core * 4 + chunk, pl.ds(me, 1)]
        return pltpu.make_async_copy(own, r1.at[chunk, pl.ds(core * CHIPS + me, 1)], self_f.at[chunk])

    def backward(chunk):
        target = pl.ds(me, 1)

        def go(chip, c, device):
            pltpu.make_async_remote_copy(
                src_ref=w2.at[chunk, pl.ds(c * CHIPS + chip, 1)], dst_ref=yb.at[core * 4 + chunk, target],
                send_sem=bwd_s.at[chunk], recv_sem=bwd_r.at[chunk], device_id=device, device_id_type=MESH,
            ).start()

        backward_self(chunk).start()
        for_others(go)

    def backward_self(chunk):
        own = w2.at[chunk, pl.ds(core * CHIPS + me, 1)]
        return pltpu.make_async_copy(own, yb.at[core * 4 + chunk, pl.ds(me, 1)], self_b.at[chunk])

    def wait_others(sem, chunk):
        most = r1.at[0, pl.ds(0, 255)]
        pltpu.make_async_copy(most, most, sem.at[chunk]).wait()

    y_forward(0)
    y_forward(4)
    pl.semaphore_wait(barrier, 128)
    pl.semaphore_signal(pair_sem, inc=1, device_id=sibling, device_id_type=MESH)
    forward(0, True)
    for load in loads[3:]:
        load.wait()
    lane = lax.broadcasted_iota(jnp.int32, (8, 128), 1)
    row8 = lax.broadcasted_iota(jnp.int32, (8, 128), 0)
    upper = (lane // 16) % 2 == 1
    par[gz] = jnp.where(
        row8 < 4,
        jnp.where(upper, damp_ref[1], damp_ref[0]),
        jnp.where(upper, blend_ref[1], blend_ref[0]),
    )
    par_copy = pltpu.make_async_remote_copy(
        src_ref=par.at[gz], dst_ref=par.at[gz], send_sem=par_s, recv_sem=par_r,
        device_id=(gx, 1 - gz), device_id_type=MESH,
    )
    par_copy.start()

    for chunk in range(1, CHUNKS):
        y_forward(chunk)
        y_forward(chunk + 4)
        forward(chunk)

    par_copy.wait()
    lane = lax.broadcasted_iota(jnp.int32, (128, 128), 1)
    mode = lax.broadcasted_iota(jnp.int32, (128, 128), 0) + 128 * (lane % 16)
    wave_x = jnp.where(mode < NX // 2, mode, mode - NX)
    wave_x = jnp.where(mode == NX // 2, 0, wave_x)
    along_x = (2.0 * math.pi / NX) * wave_x.astype(F32)
    second = (lane // 32) % 2 == 1
    for t in range(4):
        group = core * 4 + t
        slot = jnp.where(me < 64, me * 16, 8 + (me - 64) * 16)
        number = jnp.where(group == 7, slot, group + 1 + 16 * me)
        number = jnp.where(number < NY // 2, number, number - NY)
        once = jnp.logical_and(group == 7, me == 0)
        scale = jnp.where(once, 1.0, 2.0) * (1.0 / (NX * NY))
        along_y = jnp.full((128, 128), (2.0 * math.pi / NY) * number.astype(F32))
        squared = along_x * along_x + along_y * along_y
        anchor = squared == 0.0
        inverse = jnp.where(anchor, 0.0, 1.0 / jnp.where(anchor, 1.0, squared))
        cross = jnp.where(second, along_x, along_y)
        straight = jnp.where(anchor, 1.0, cross * cross * inverse) * scale
        mixed = -along_x * along_y * inverse * scale
        for half in range(2):
            damper = jnp.exp(-par[half, 0:1, :] * squared)
            coef[t, half, 0] = straight * damper
            coef[t, half, 1] = mixed * damper
    level_row = lax.broadcasted_iota(jnp.int32, (256, 256), 0)
    level_row = level_row // 128 * 2 + (level_row // 16) % 2
    weight = jnp.zeros((256, 256), F32)
    for level in range(4):
        value = jnp.max(par[level // 2, 4:5, (level % 2) * 16 : (level % 2) * 16 + 16])
        weight = jnp.where(level_row == level, value, weight)
    high, low = split(vert_ref[0] * weight + vert_ref[1] * (1.0 - weight))
    vmat[0] = high
    vmat[1] = low

    sign = jnp.where(lane < 64, 1.0, -1.0)

    def spun(value):
        return pltpu.roll(value, 64, axis=1)

    def doubled(first, second):
        top = jnp.concatenate([first, second], axis=1)
        bottom = jnp.concatenate([spun(first) * sign, spun(second) * sign], axis=1)
        return split(jnp.concatenate([top, bottom], axis=0))

    def column(t):
        halves = [
            jnp.concatenate([r1[t, h * 64 : h * 64 + 64], r1[t, CHIPS + h * 64 : CHIPS + h * 64 + 64]], axis=0)
            for h in range(2)
        ]
        high, low = doubled(*halves)
        step = dot_const_left((slabf_ref[0], slabf_ref[1]), high, low)
        turned = []
        for h in range(2):
            part = step[:, h * 128 : h * 128 + 128]
            turned.append(part * twid_ref[0] + spun(part) * twid_ref[1])
        high, low = split(jnp.concatenate(turned, axis=0))
        modes = dot_const_right(high, low, (mix_ref[0], mix_ref[1]))
        kept = []
        for h in range(2):
            rows = slice(h * 128, h * 128 + 128)
            kept.append(modes[rows, :128] * coef[t, h, 0] + modes[rows, 128:] * coef[t, h, 1])
        high, low = split(jnp.concatenate(kept, axis=1))
        back = dot_const_right(high, low, (vmat[0], vmat[1]))
        turned = []
        for h in range(2):
            part = back[:, h * 128 : h * 128 + 128]
            turned.append(part * twid_ref[0] - spun(part) * twid_ref[1])
        high, low = doubled(*turned)
        result = dot_const_left((slabi_ref[0], slabi_ref[1]), high, low)
        for h in range(2):
            for c in range(2):
                w2[t, c * CHIPS + h * 64 : c * CHIPS + h * 64 + 64] = result[c * 64 : c * 64 + 64, h * 128 : h * 128 + 128]

    for chunk in range(CHUNKS):
        wait_others(fwd_r, chunk)
        forward_self(chunk).wait()
        column(chunk)
        backward(chunk)

    def y_backward(group):
        data = yb[group].T
        high, low = split(data)
        if group < 7:
            c = group + 1
            full = dot_const_right(high, low, (main_ref[0, group], main_ref[1, group]))
            real = full[:64, :128] + full[64:, 128:]
            imag = full[64:, :128] - full[:64, 128:]
            for a in range(9):
                factor = math.cos(2.0 * math.pi * a * c / 16)
                acc_e[a] = factor * real if group == 0 else acc_e[a] + factor * real
            for a in range(1, 8):
                factor = math.sin(2.0 * math.pi * a * c / 16)
                acc_o[a] = factor * imag if group == 0 else acc_o[a] + factor * imag
        else:
            both = dot_const_right(high[:64], low[:64], (packed_ref[0, :, :256], packed_ref[1, :, :256]))
            both = both + dot_const_right(high[64:], low[64:], (packed_ref[0, :, 256:], packed_ref[1, :, 256:]))
            for a in range(9):
                acc_e[a] = acc_e[a] + (both[:, :128] + (-1.0) ** a * both[:, 128:])

    for chunk in range(CHUNKS):
        wait_others(bwd_r, chunk)
        backward_self(chunk).wait()
        y_backward(chunk)
        y_backward(chunk + 4)

    out_ref[:, 0:128] = acc_e[0]
    out_ref[:, 1024:1152] = acc_e[8]
    for a in range(1, 8):
        out_ref[:, a * 128 : a * 128 + 128] = acc_e[a] - acc_o[a]
        out_ref[:, (16 - a) * 128 : (16 - a) * 128 + 128] = acc_e[a] + acc_o[a]

    for chunk in range(CHUNKS):
        wait_others(fwd_s, chunk)
        wait_others(bwd_s, chunk)


def body(cotangent, damping, blending):
    consts = [jnp.asarray(table) for table in tables()]
    anywhere = pl.BlockSpec(memory_space=pltpu.HBM)
    dma = pltpu.SemaphoreType.DMA
    scratch = [
        ((16, 64, 128), F32),
        ((8, 128, 128), F32),
        ((CHUNKS, 2 * CHIPS, 128), F32),
        ((4, 2, 2, 128, 128), F32),
        ((2, 256, 256), BF16),
        ((CHUNKS, 2 * CHIPS, 128), F32),
        ((8, 128, 128), F32),
        ((9, 64, 128), F32),
        ((8, 64, 128), F32),
        ((2, 8, 128), F32),
    ]
    result = pl.pallas_call(
        kernel,
        out_shape=jax.ShapeDtypeStruct((64, NY), F32),
        in_specs=[anywhere] * (3 + len(consts)),
        out_specs=pl.BlockSpec(memory_space=pltpu.VMEM),
        scratch_shapes=[pltpu.VMEM((64, NY), F32), pltpu.SMEM((2,), F32), pltpu.SMEM((2,), F32)]
        + [pltpu.VMEM(c.shape, c.dtype) for c in consts]
        + [pltpu.VMEM(*s) for s in scratch]
        + [dma((CHUNKS,))] * 4
        + [dma, dma, dma((CHUNKS,)), dma((CHUNKS,)), dma((3 + len(consts),)), pltpu.SemaphoreType.REGULAR],
        compiler_params=pltpu.CompilerParams(
            collective_id=0, has_side_effects=True, vmem_limit_bytes=62 * 1024 * 1024
        ),
    )(cotangent.reshape(64, NY), damping, blending, *consts)
    return result.reshape(2, 2, 16, NY)


def solution(mesh):
    return jax.shard_map(
        body,
        mesh=mesh,
        in_specs=(P(None, "gz", "gx", None), P("gz"), P("gz")),
        out_specs=P(None, "gz", "gx", None),
        check_vma=False,
    )
```
